256 devices in a mesh: curve: 32 (over z, y), group: 8 (over x, core).
Axes of the slice: x: 4, y: 4, z: 8, core: 2. Of those that a mesh axis runs over, the one named last changes fastest.
Arguments:
- state: float32 [2560, 20, 16, 256], P(('curve', 'group')), may hold values from -6 to 6
- coarse_state: float32 [2560, 20, 640], P(('curve', 'group')), may hold values from -6 to 6
- coarse_kappa: float32 [2560, 20, 640], P(('curve', 'group')), may hold values from 0.03 to 0.16
- bound_shift: int32 [8, 32], P('group'), may hold values from -5 to 5, as said below
Outputs:
- new_state: float32 [5120, 20, 16, 256], P(('curve', 'group'))
The draws below stay inside these ranges and needn't reach their ends.
Inputs may be any that keep to these rules, and one draw needn't show every extreme that they name: The last entry of every row is 0. In every row some device c with 1 <= c <= 32 - 2 has bound_shift[g, c - 1] = -5 and bound_shift[g, c] = 5, so it holds 20 patches after the regrid.
All inputs are finite; a program needn't handle non-finite values.
Results may differ from the reference program's by a relative error of at most 0.000094.
Values sent between devices are 32-bit elements; how exact they have to be, the bound alone decides.
A program may use at most 128 MiB of HBM per device.

```python
import math
import jax
import jax.numpy as jnp
from jax import lax

SPEC = 20
PC = 16
CH = 8
CX = 10
P_DEV = 10
PATCHES = 2560
N_CURVE = 32
N_GROUP = 8


def draw_bound_shift(key, part):
    half_count = P_DEV // 2
    first_key, second_key = jax.random.split(jax.random.fold_in(key, 17))
    shifts = jax.random.randint(first_key, (N_GROUP, N_CURVE), -half_count, half_count + 1)
    widest = jax.random.randint(second_key, (N_GROUP, 1), 1, N_CURVE - 1)
    columns = jnp.arange(N_CURVE, dtype=jnp.int32)[None, :]
    shifts = jnp.where(columns == widest - 1, -half_count, shifts)
    shifts = jnp.where(columns == widest, half_count, shifts)
    shifts = jnp.where(columns == N_CURVE - 1, 0, shifts)
    return shifts.astype(jnp.int32)


def level_of(key, extent, cuts, least, high):
    loudness, own = 1.0, jax.random.fold_in(key, 6)
    for dim, blocks in cuts:
        heights = jnp.exp(jax.random.uniform(jax.random.fold_in(own, dim), (blocks,), jnp.float32, least / len(cuts), high / len(cuts)))
        loudness = loudness * jnp.repeat(heights, extent[dim] // blocks).reshape([-1 if axis == dim else 1 for axis in range(len(extent))])
    return loudness


def centred(key, extent, spread, most, shards=(), kind=jnp.bfloat16):
    values = jax.random.normal(key, extent, jnp.float32) * spread
    if len(shards) > 0:
        values = level_of(key, extent, shards, -0.22, 0.18) * values
    return jnp.clip(values, min=-most, max=most).astype(kind)


def setup_inputs(seed: int = 0) -> dict:
    key_of = jax.random.split(jax.random.key(seed), 5)
    return {
        "state": centred(key_of[0], (PATCHES, SPEC, PC, PC * PC), 1.0, 6.0, ((0, 256),), jnp.float32),
        "coarse_state": centred(key_of[1], (PATCHES, SPEC, CX * CH * CH), 1.0, 6.0, ((0, 256),), jnp.float32),
        "coarse_kappa": jnp.clip(jnp.exp(math.log(0.16) - 1.6739764 * jax.random.uniform(key_of[2], (PATCHES, SPEC, CX * CH * CH), jnp.float32) ** level_of(key_of[2], (PATCHES, SPEC, CX * CH * CH), ((0, 256),), -0.2, 0.2)), 0.03, 0.16),
        "bound_shift": draw_bound_shift(jax.random.fold_in(key_of[4], 71), 0),
    }


def refine_block(outer_block):
    refined = jnp.repeat(jnp.repeat(jnp.repeat(outer_block, 2, axis=1), 2, axis=2), 2, axis=3)
    return refined[:, 1:-1, 1:-1, 1:-1]


def neighbour(values, axis_dim, begin_at, edge_cells):
    pieces = [slice(None), slice(1, -1), slice(1, -1), slice(1, -1)]
    pieces[axis_dim] = slice(begin_at, begin_at + edge_cells)
    return values[tuple(pieces)]


def diffuse_patch(patch_cells, outer_state, outer_kappa):
    species = patch_cells.shape[0]
    edge_cells = patch_cells.shape[1]
    inside = patch_cells.reshape(species, edge_cells, edge_cells, edge_cells)
    padded = refine_block(outer_state)
    padded = padded.at[:, 1:-1, 1:-1, 1:-1].set(inside)
    kappa_fine = refine_block(outer_kappa)
    center = padded[:, 1:-1, 1:-1, 1:-1]
    kappa_center = kappa_fine[:, 1:-1, 1:-1, 1:-1]
    change = jnp.zeros_like(center)
    for axis_dim in (1, 2, 3):
        for begin_at in (0, 2):
            near_cells = neighbour(padded, axis_dim, begin_at, edge_cells)
            near_kappa = neighbour(kappa_fine, axis_dim, begin_at, edge_cells)
            change = change + 0.5 * (kappa_center + near_kappa) * (near_cells - center)
    return (center + change).reshape(species, edge_cells, edge_cells * edge_cells)


def extend_group(grid, group_id):
    own_block = grid[group_id]
    lower_plane = grid[(group_id - 1) % N_GROUP][:, :, :, CH - 1:CH, :]
    upper_plane = grid[(group_id + 1) % N_GROUP][:, :, :, 0:1, :]
    widened = jnp.concatenate([lower_plane, own_block, upper_plane], axis=3)
    below_plane = jnp.roll(widened, 1, axis=0)[..., CH - 1:CH]
    above_plane = jnp.roll(widened, -1, axis=0)[..., 0:1]
    return jnp.concatenate([below_plane, widened, above_plane], axis=4)


def to_grid(blocks):
    shaped = blocks.reshape(N_CURVE, N_GROUP, P_DEV, SPEC, CX, CH, CH)
    shaped = jnp.transpose(shaped, (1, 0, 2, 3, 4, 5, 6))
    return shaped.reshape(N_GROUP, N_CURVE * P_DEV, SPEC, CX, CH, CH)


def reference(state, coarse_state, coarse_kappa, bound_shift):
    column_len = N_CURVE * P_DEV
    grid_state = to_grid(coarse_state)
    grid_kappa = to_grid(coarse_kappa)
    shaped = state.reshape(N_CURVE, N_GROUP, P_DEV, SPEC, PC, PC * PC)
    slot_index = jnp.arange(2 * P_DEV, dtype=jnp.int32)
    curve_ids = jnp.arange(N_CURVE, dtype=jnp.int32)

    def one_patch(items):
        patch_cells, outer_state, outer_kappa = items
        return diffuse_patch(patch_cells, outer_state, outer_kappa)

    results = []
    for group_id in range(N_GROUP):
        column = shaped[:, group_id].reshape(column_len, SPEC, PC, PC * PC)
        outer_state = extend_group(grid_state, group_id)
        outer_kappa = extend_group(grid_kappa, group_id)
        smoothed = lax.map(one_patch, (column, outer_state, outer_kappa))
        shifts = bound_shift[group_id]
        before = jnp.concatenate([jnp.zeros((1,), jnp.int32), shifts[:-1]])
        counts = P_DEV + shifts - before
        positions = curve_ids[:, None] * P_DEV + before[:, None] + slot_index[None, :]
        positions = jnp.clip(positions, 0, column_len - 1).astype(jnp.int32)
        slot_valid = slot_index[None, :] < counts[:, None]
        picked = smoothed[positions]
        picked = jnp.where(slot_valid[:, :, None, None, None], picked, jnp.zeros((), smoothed.dtype))
        results.append(picked)
    stacked = jnp.stack(results, axis=1)
    return stacked.reshape(N_CURVE * N_GROUP * 2 * P_DEV, SPEC, PC, PC * PC)
```

```python
import jax
import jax.numpy as jnp
import numpy as np
from jax import lax
from jax.experimental import pallas as pl
from jax.experimental.pallas import tpu as pltpu
from jax.sharding import PartitionSpec as P

MESH = pl.DeviceIdType.MESH
SPEC = 20
EDGE = 16
LANES = EDGE * EDGE
PATCHES = 10
HALF = 5
COARSE = 640
PITCH = 24
TILES = COARSE // 128
DEPTH = 256
CHUNK = 10
ROWS = CHUNK * EDGE
CHUNKS = SPEC // CHUNK
BLOCK = 2


def row_tables():
    own = np.zeros((SPEC * EDGE, DEPTH), np.float32)
    outer = np.zeros_like(own)
    face = np.zeros_like(own)
    for s in range(SPEC):
        for i in range(EDGE):
            half = i // 2
            own[s * EDGE + i, (half + 1) * PITCH + s] = 1.0
            outer[s * EDGE + i, (half + 2 if i % 2 else half) * PITCH + s] = 1.0
            if i == 0:
                face[s * EDGE + i, s] = 1.0
            if i == EDGE - 1:
                face[s * EDGE + i, 9 * PITCH + s] = 1.0
    return np.stack([own, outer, face])


def lane_tables():
    half = np.zeros((64, LANES), np.float32)
    y_own, y_side, y_face = np.zeros_like(half), np.zeros_like(half), np.zeros_like(half)
    z_own, z_side, z_face = np.zeros_like(half), np.zeros_like(half), np.zeros_like(half)
    for r in range(EDGE):
        for q in range(EDGE):
            lane, cy, cz = r * EDGE + q, r // 2, q // 2
            here = cy * 8 + cz
            half[here, lane] = 0.5
            y_own[here, lane] += 0.5
            z_own[here, lane] += 0.5
            near = r + 1 if r % 2 else r - 1
            if near < 0:
                y_side[56 + cz, lane], y_face[56 + cz, lane] = 0.5, 1.0
            elif near >= EDGE:
                y_side[cz, lane], y_face[cz, lane] = 0.5, 1.0
            else:
                y_own[near // 2 * 8 + cz, lane] += 0.5
            near = q + 1 if q % 2 else q - 1
            if near < 0:
                z_side[cy * 8 + 7, lane], z_face[cy * 8 + 7, lane] = 0.5, 1.0
            elif near >= EDGE:
                z_side[cy * 8, lane], z_face[cy * 8, lane] = 0.5, 1.0
            else:
                z_own[cy * 8 + near // 2, lane] += 0.5
    parts = [half, y_side, y_own, z_own, z_side, y_face, z_face, 2.0 * half]
    return np.concatenate([np.concatenate([part, part]) for part in parts])


def lane_iota(rows):
    return lax.broadcasted_iota(jnp.int32, (rows, 128), 1)


def stage_tile(tile, values, target, pick):
    lane = lane_iota(SPEC)
    high = values.astype(jnp.bfloat16).astype(jnp.float32)
    rest = values - high
    even = jnp.where(lane < 64, high, pltpu.roll(rest, 64, 1))
    odd = jnp.where(lane < 64, pltpu.roll(high, 64, 1), rest)
    target[pick, 2 * tile * PITCH : 2 * tile * PITCH + SPEC, :] = even
    target[pick, (2 * tile + 1) * PITCH : (2 * tile + 1) * PITCH + SPEC, :] = odd


def exchange_kernel(
    state_ref,
    coarse_state_ref,
    coarse_kappa_ref,
    rows_ref,
    lanes_ref,
    own_ref,
    left_ref,
    right_ref,
    cells,
    coarse,
    row_mats,
    lane_mats,
    staged,
    sides,
    pack_out,
    pack_in,
    edge_out,
    edge_in,
    weights,
    cell_sem,
    coarse_sem,
    table_sem,
    pack_send,
    pack_recv,
    edge_send,
    edge_recv,
    move_send,
    move_recv,
):
    curve = lax.axis_index("curve")
    group = lax.axis_index("group")
    n_curve = lax.axis_size("curve")
    n_group = lax.axis_size("group")
    ahead = (lax.rem(curve + 1, n_curve), group)
    behind = (lax.rem(curve + n_curve - 1, n_curve), group)
    above = (curve, lax.rem(group + 1, n_group))
    below = (curve, lax.rem(group + n_group - 1, n_group))

    def load_coarse(field, part, begin, count):
        source = (coarse_state_ref, coarse_kappa_ref)[field]
        return pltpu.make_async_copy(
            source.at[pl.ds(begin, count)],
            coarse.at[field, pl.ds(begin + 1, count)],
            coarse_sem.at[field, part],
        )

    def load_cells(patch):
        return pltpu.make_async_copy(state_ref.at[patch], cells.at[patch], cell_sem.at[patch])

    def load_tables():
        return (
            pltpu.make_async_copy(rows_ref, row_mats, table_sem.at[0]),
            pltpu.make_async_copy(lanes_ref, lane_mats, table_sem.at[1]),
        )

    parts = ((3, 4), (0, 3), (7, 3))
    for field in range(2):
        load_coarse(field, 0, *parts[0]).start()
    for copy in load_tables():
        copy.start()
    for patch in (5, 4):
        load_cells(patch).start()
    for part in (1, 2):
        for field in range(2):
            load_coarse(field, part, *parts[part]).start()
    for patch in (6, 3, 7, 2, 8, 1, 9, 0):
        load_cells(patch).start()

    barrier = pltpu.get_barrier_semaphore()
    for device in (above, below, ahead, behind):
        pl.semaphore_signal(barrier, inc=1, device_id=device, device_id_type=MESH)

    staged[...] = jnp.zeros_like(staged)
    sides[...] = jnp.zeros_like(sides)

    lane = lane_iota(SPEC)
    row_of = (lane % 64) // 8

    def pack(slot, patches, first):
        for tile in range(TILES):
            up = jnp.zeros((SPEC, 128), jnp.float32)
            down = jnp.zeros((SPEC, 128), jnp.float32)
            for place, patch in enumerate(patches):
                for field in range(2):
                    j = (first + place) * 2 + field
                    values = coarse[field, patch + 1, :, tile * 128 : (tile + 1) * 128]
                    up = jnp.where(row_of == 7 - j, pltpu.roll(values, (128 - 8 * j) % 128, 1), up)
                    down = jnp.where(row_of == j, pltpu.roll(values, 8 * j, 1), down)
            pack_out[0, slot, :, tile * 128 : (tile + 1) * 128] = up
            pack_out[1, slot, :, tile * 128 : (tile + 1) * 128] = down

    def pack_copy(way, slot):
        return pltpu.make_async_remote_copy(
            src_ref=pack_out.at[way, slot],
            dst_ref=pack_in.at[way, slot],
            send_sem=pack_send.at[way, slot],
            recv_sem=pack_recv.at[way, slot],
            device_id=(above, below)[way],
            device_id_type=MESH,
        )

    def edge_copy(way):
        return pltpu.make_async_remote_copy(
            src_ref=edge_out.at[way],
            dst_ref=edge_in.at[way],
            send_sem=edge_send.at[way],
            recv_sem=edge_recv.at[way],
            device_id=(ahead, behind)[way],
            device_id_type=MESH,
        )

    def move_copy(way, k, chunk):
        patch = 5 + k if way == 0 else 4 - k
        slot = k if way == 0 else 4 - k
        part = pl.ds(chunk * CHUNK, CHUNK)
        return pltpu.make_async_remote_copy(
            src_ref=own_ref.at[patch, part],
            dst_ref=(left_ref, right_ref)[way].at[slot, part],
            send_sem=move_send.at[way, k, chunk],
            recv_sem=move_recv.at[way, k, chunk],
            device_id=(ahead, behind)[way],
            device_id_type=MESH,
        )

    def stage(slot):
        for field in range(2):
            for tile in range(TILES):
                values = coarse[field, slot, :, tile * 128 : (tile + 1) * 128]
                stage_tile(tile, values, staged.at[field], slot)

    for field in range(2):
        load_coarse(field, 0, *parts[0]).wait()
    pack(0, (5, 4), 2)
    pl.semaphore_wait(barrier, 4)
    for way in range(2):
        pack_copy(way, 0).start()
    stage(5)
    stage(6)
    for copy in load_tables():
        copy.wait()

    def smooth_chunk(patch, chunk, factors, kappa_own, state_own):
        begin = pl.multiple_of(chunk * ROWS, ROWS)
        rows = [row_mats[t, pl.ds(begin, ROWS), :] for t in range(3)]

        def table(first, count):
            return lane_mats[first * 128 : (first + count) * 128, :]

        def dot(a, b):
            return jnp.dot(a, b, preferred_element_type=jnp.float32)

        spread = dot(rows[0], factors).astype(jnp.bfloat16)
        outer = dot(rows[1], kappa_own).astype(jnp.bfloat16)
        face = dot(rows[2], state_own).astype(jnp.bfloat16)
        weights[0] = dot(spread[:, 128:256], table(0, 1))
        weights[1] = dot(outer, table(0, 1))
        weights[2] = dot(spread[:, 0:256], table(1, 2))
        weights[3] = dot(spread[:, 128:384], table(3, 2))
        weights[4] = dot(spread[:, 384:512], table(5, 1))
        weights[5] = dot(spread[:, 512:640], table(6, 1))
        weights[6] = dot(face, table(7, 1))

        shape = (BLOCK, EDGE, LANES)
        x = lax.broadcasted_iota(jnp.int32, shape, 1)
        lanes = lax.broadcasted_iota(jnp.int32, shape, 2)
        y, z = lanes // EDGE, lanes % EDGE

        def block(b, carry):
            species = chunk * CHUNK + b * BLOCK
            p = cells[patch, pl.ds(species, BLOCK)]
            at = pl.ds(pl.multiple_of(b * BLOCK * EDGE, BLOCK * EDGE), BLOCK * EDGE)
            half, half_outer, w_y, w_z, u_y, u_z, u_x = (
                weights[t, at, :].reshape(shape) for t in range(7)
            )

            def pair(index, axis, step, extent, outside):
                up = pltpu.roll(p, extent - step, axis)
                down = pltpu.roll(p, step, axis)
                odd = index % 2 == 1
                inner = jnp.where(odd, down, up)
                far = jnp.where(odd, up, down)
                far = jnp.where((index == 0) | (index == EDGE - 1), outside, far)
                return inner, far

            in_x, out_x = pair(x, 1, 1, EDGE, u_x)
            in_y, out_y = pair(y, 2, EDGE, LANES, u_y)
            in_z, out_z = pair(z, 2, 1, LANES, u_z)
            change = half * (2.0 * (in_x + in_y + in_z) - 6.0 * p)
            change = change + (half + half_outer) * (out_x - p)
            change = change + w_y * (out_y - p)
            change = change + w_z * (out_z - p)
            own_ref[patch, pl.ds(species, BLOCK)] = p + change
            return carry

        lax.fori_loop(0, CHUNK // BLOCK, block, 0)

    def smooth(way, k):
        patch = 5 + k if way == 0 else 4 - k
        slot = (k + 1) // 2
        base = 2 * lax.rem(k + 1, 2) + way
        for field in range(2):
            j = base * 2 + field
            back = 8 * j
            forth = lax.rem(128 - 8 * j, 128)
            for tile in range(TILES):
                part = slice(tile * 128, (tile + 1) * 128)
                low = pltpu.roll(pack_in[0, slot, :, part], back, 1)
                high = pltpu.roll(pack_in[1, slot, :, part], forth, 1)
                values = jnp.where(row_of == 7, low, jnp.where(row_of == 0, high, 0.0))
                stage_tile(tile, values, sides, field)
        z = lane_iota(DEPTH) % 8

        def across(field):
            low, high = staged[field, patch], staged[field, patch + 2]
            return jnp.where(z == 7, low, jnp.where(z == 0, high, 0.0)).astype(jnp.bfloat16)

        state_own = staged[0, patch + 1].astype(jnp.bfloat16)
        kappa_own = staged[1, patch + 1].astype(jnp.bfloat16)
        factors = jnp.concatenate(
            [
                sides[1].astype(jnp.bfloat16),
                kappa_own,
                across(1),
                sides[0].astype(jnp.bfloat16),
                across(0),
            ],
            axis=1,
        )
        load_cells(patch).wait()
        for chunk in range(CHUNKS):
            smooth_chunk(patch, chunk, factors, kappa_own, state_own)
            move_copy(way, k, chunk).start()

    def step(k, carry):
        @pl.when(k == 0)
        def _():
            for way in range(2):
                pack_copy(way, 0).wait_recv()

        @pl.when(k == 1)
        def _():
            for way in range(2):
                pack_copy(way, 1).wait_recv()

        @pl.when(k == 3)
        def _():
            for way in range(2):
                pack_copy(way, 2).wait_recv()

        @pl.when(k == 4)
        def _():
            for way in range(2):
                edge_copy(way).wait_recv()
            for field in range(2):
                for tile in range(TILES):
                    part = slice(tile * 128, (tile + 1) * 128)
                    low = pltpu.roll(edge_in[0, field], (7 - tile) % 128, 1)
                    high = pltpu.roll(edge_in[1, field], (128 - tile) % 128, 1)
                    coarse[field, 0, :, part] = low
                    coarse[field, 11, :, part] = high

        stage(7 + k)
        stage(4 - k)
        smooth(0, k)
        smooth(1, k)

        @pl.when(k == 0)
        def _():
            for part in (1, 2):
                for field in range(2):
                    load_coarse(field, part, *parts[part]).wait()
            pack(1, (6, 3, 7, 2), 0)
            pack(2, (8, 1, 9, 0), 0)
            for field in range(2):
                up = jnp.zeros((SPEC, 128), jnp.float32)
                down = jnp.zeros((SPEC, 128), jnp.float32)
                for tile in range(TILES):
                    part = slice(tile * 128, (tile + 1) * 128)
                    last = coarse[field, PATCHES, :, part]
                    first = coarse[field, 1, :, part]
                    up = jnp.where(lane % 8 == tile, pltpu.roll(last, (128 + tile - 7) % 128, 1), up)
                    down = jnp.where(lane % 8 == tile, pltpu.roll(first, tile, 1), down)
                edge_out[0, field] = up
                edge_out[1, field] = down
            for way in range(2):
                pack_copy(way, 1).start()
                pack_copy(way, 2).start()
                edge_copy(way).start()

        return carry

    lax.fori_loop(0, HALF, step, 0)

    for way in range(2):
        for slot in range(3):
            pack_copy(way, slot).wait_send()
        edge_copy(way).wait_send()
        for k in range(HALF):
            for chunk in range(CHUNKS):
                move_copy(way, k, chunk).wait()


def place_kernel(shift_ref, own_ref, left_ref, right_ref, out_ref, zeros, sem):
    curve = lax.axis_index("curve")
    here = shift_ref[0, curve]
    before = jnp.where(curve > 0, shift_ref[0, jnp.maximum(curve - 1, 0)], 0)
    count = PATCHES + here - before
    zeros[...] = jnp.zeros_like(zeros)
    for slot in range(2 * PATCHES):
        position = before + slot
        used = slot < count
        target = out_ref.at[slot]

        def put(source):
            pltpu.make_async_copy(source, target, sem).start()

        @pl.when(used & (position < 0))
        def _():
            put(left_ref.at[jnp.clip(position + HALF, 0, HALF - 1)])

        @pl.when(used & (position >= PATCHES))
        def _():
            put(right_ref.at[jnp.clip(position - PATCHES, 0, HALF - 1)])

        @pl.when(used & (position >= 0) & (position < PATCHES))
        def _():
            put(own_ref.at[jnp.clip(position, 0, PATCHES - 1)])

        @pl.when(jnp.logical_not(used))
        def _():
            put(zeros)

    pltpu.make_async_copy(out_ref, out_ref, sem).wait()


def shards(state, coarse_state, coarse_kappa, bound_shift):
    f32, bf16 = jnp.float32, jnp.bfloat16
    patch = (SPEC, EDGE, LANES)
    hbm = pl.BlockSpec(memory_space=pltpu.HBM)
    vmem = pl.BlockSpec(memory_space=pltpu.VMEM)
    row_table = jnp.asarray(row_tables(), bf16)
    lane_table = jnp.asarray(lane_tables(), bf16)
    own, left, right = pl.pallas_call(
        exchange_kernel,
        name="exchange",
        out_shape=[
            jax.ShapeDtypeStruct((count,) + patch, f32) for count in (PATCHES, HALF, HALF)
        ],
        in_specs=[hbm] * 5,
        out_specs=[vmem] * 3,
        scratch_shapes=[
            pltpu.VMEM((PATCHES,) + patch, f32),
            pltpu.VMEM((2, PATCHES + 2, SPEC, COARSE), f32),
            pltpu.VMEM(row_table.shape, bf16),
            pltpu.VMEM(lane_table.shape, bf16),
            pltpu.VMEM((2, PATCHES + 2, DEPTH, 128), f32),
            pltpu.VMEM((2, DEPTH, 128), f32),
            pltpu.VMEM((2, 3, SPEC, COARSE), f32),
            pltpu.VMEM((2, 3, SPEC, COARSE), f32),
            pltpu.VMEM((2, 2, SPEC, 128), f32),
            pltpu.VMEM((2, 2, SPEC, 128), f32),
            pltpu.VMEM((7, ROWS, LANES), f32),
            pltpu.SemaphoreType.DMA((PATCHES,)),
            pltpu.SemaphoreType.DMA((2, 3)),
            pltpu.SemaphoreType.DMA((2,)),
            pltpu.SemaphoreType.DMA((2, 3)),
            pltpu.SemaphoreType.DMA((2, 3)),
            pltpu.SemaphoreType.DMA((2,)),
            pltpu.SemaphoreType.DMA((2,)),
            pltpu.SemaphoreType.DMA((2, HALF, CHUNKS)),
            pltpu.SemaphoreType.DMA((2, HALF, CHUNKS)),
        ],
        compiler_params=pltpu.CompilerParams(
            collective_id=0, has_side_effects=True, vmem_limit_bytes=36 << 20
        ),
        cost_estimate=pl.CostEstimate(flops=8 << 30, bytes_accessed=12 << 20, transcendentals=0),
    )(state, coarse_state, coarse_kappa, row_table, lane_table)
    return pl.pallas_call(
        place_kernel,
        name="place",
        out_shape=jax.ShapeDtypeStruct((2 * PATCHES,) + patch, f32),
        in_specs=[pl.BlockSpec(memory_space=pltpu.SMEM)] + [vmem] * 3,
        out_specs=hbm,
        scratch_shapes=[pltpu.VMEM(patch, f32), pltpu.SemaphoreType.DMA],
        compiler_params=pltpu.CompilerParams(vmem_limit_bytes=16 << 20),
        cost_estimate=pl.CostEstimate(flops=0, bytes_accessed=7 << 20, transcendentals=0),
    )(bound_shift, own, left, right)


def solution(mesh):
    in_specs = (
        P(("curve", "group"), None, None, None),
        P(("curve", "group"), None, None),
        P(("curve", "group"), None, None),
        P("group", None),
    )
    out_specs = P(("curve", "group"), None, None, None)
    return jax.shard_map(shards, mesh=mesh, in_specs=in_specs, out_specs=out_specs, check_vma=False)
```

```python
import jax
import jax.numpy as jnp
import numpy as np
from jax import lax
from jax.experimental import pallas as pl
from jax.experimental.pallas import tpu as pltpu
from jax.sharding import PartitionSpec as P

MESH = pl.DeviceIdType.MESH
SPEC = 20
EDGE = 16
LANES = EDGE * EDGE
PATCHES = 10
HALF = 5
COARSE = 640
PITCH = 24
TILES = COARSE // 128
CHUNK = 10
CHUNKS = SPEC // CHUNK
BLOCK = 2
FLAT = SPEC * 8


def lane_tables():
    half = np.zeros((64, LANES), np.float32)
    y_own, y_side, y_face = np.zeros_like(half), np.zeros_like(half), np.zeros_like(half)
    z_own, z_side, z_face = np.zeros_like(half), np.zeros_like(half), np.zeros_like(half)
    for r in range(EDGE):
        for q in range(EDGE):
            lane, cy, cz = r * EDGE + q, r // 2, q // 2
            here = cy * 8 + cz
            half[here, lane] = 0.5
            y_own[here, lane] += 0.5
            z_own[here, lane] += 0.5
            near = r + 1 if r % 2 else r - 1
            if near < 0:
                y_side[56 + cz, lane], y_face[56 + cz, lane] = 0.5, 1.0
            elif near >= EDGE:
                y_side[cz, lane], y_face[cz, lane] = 0.5, 1.0
            else:
                y_own[near // 2 * 8 + cz, lane] += 0.5
            near = q + 1 if q % 2 else q - 1
            if near < 0:
                z_side[cy * 8 + 7, lane], z_face[cy * 8 + 7, lane] = 0.5, 1.0
            elif near >= EDGE:
                z_side[cy * 8, lane], z_face[cy * 8, lane] = 0.5, 1.0
            else:
                z_own[cy * 8 + near // 2, lane] += 0.5
    parts = [half, half, y_own, y_side, z_own, z_side, y_face, z_face, 2.0 * half]
    return np.concatenate([np.concatenate([part, part]) for part in parts])


def lane_iota(rows):
    return lax.broadcasted_iota(jnp.int32, (rows, 128), 1)


def split_pair(values):
    lane = lane_iota(SPEC)
    high = values.astype(jnp.bfloat16).astype(jnp.float32)
    rest = values - high
    even = jnp.where(lane < 64, high, pltpu.roll(rest, 64, 1))
    odd = jnp.where(lane < 64, pltpu.roll(high, 64, 1), rest)
    return even, odd


def put_rows(target, place, values):
    if 0 <= place < 8:
        target[pl.ds(place, SPEC, stride=8), :] = values


def exchange_kernel(
    state_ref,
    coarse_state_ref,
    coarse_kappa_ref,
    lanes_ref,
    own_ref,
    left_ref,
    right_ref,
    cells,
    coarse,
    lane_mats,
    staged,
    outer,
    sides,
    faces,
    face_rows,
    pack_out,
    pack_in,
    edge_out,
    edge_in,
    weights,
    fix_out,
    fix_in,
    cell_sem,
    coarse_sem,
    table_sem,
    pack_send,
    pack_recv,
    edge_send,
    edge_recv,
    move_send,
    move_recv,
    fix_send,
    fix_recv,
):
    curve = lax.axis_index("curve")
    group = lax.axis_index("group")
    n_curve = lax.axis_size("curve")
    n_group = lax.axis_size("group")
    ahead = (lax.rem(curve + 1, n_curve), group)
    behind = (lax.rem(curve + n_curve - 1, n_curve), group)
    above = (curve, lax.rem(group + 1, n_group))
    below = (curve, lax.rem(group + n_group - 1, n_group))

    def load_coarse(field, part, begin, count):
        source = (coarse_state_ref, coarse_kappa_ref)[field]
        return pltpu.make_async_copy(
            source.at[pl.ds(begin, count)],
            coarse.at[field, pl.ds(begin + 1, count)],
            coarse_sem.at[field, part],
        )

    def load_cells(patch):
        return pltpu.make_async_copy(state_ref.at[patch], cells.at[patch], cell_sem.at[patch])

    def load_table():
        return pltpu.make_async_copy(lanes_ref, lane_mats, table_sem)

    parts = ((3, 4), (0, 3), (7, 3))
    for field in range(2):
        load_coarse(field, 0, *parts[0]).start()
    load_table().start()
    for patch in (5, 4):
        load_cells(patch).start()
    for part in (1, 2):
        for field in range(2):
            load_coarse(field, part, *parts[part]).start()
    for patch in (6, 3, 7, 2, 8, 1, 9, 0):
        load_cells(patch).start()

    barrier = pltpu.get_barrier_semaphore()
    for device in (above, below, ahead, behind):
        pl.semaphore_signal(barrier, inc=1, device_id=device, device_id_type=MESH)

    faces[...] = jnp.zeros_like(faces)

    lane = lane_iota(SPEC)
    row_of = (lane % 64) // 8

    def pack(slot, patches, first):
        for tile in range(TILES):
            up = jnp.zeros((SPEC, 128), jnp.float32)
            down = jnp.zeros((SPEC, 128), jnp.float32)
            for place, patch in enumerate(patches):
                for field in range(2):
                    j = (first + place) * 2 + field
                    values = coarse[field, patch + 1, :, tile * 128 : (tile + 1) * 128]
                    up = jnp.where(row_of == 7 - j, pltpu.roll(values, (128 - 8 * j) % 128, 1), up)
                    down = jnp.where(row_of == j, pltpu.roll(values, 8 * j, 1), down)
            pack_out[0, slot, :, tile * 128 : (tile + 1) * 128] = up
            pack_out[1, slot, :, tile * 128 : (tile + 1) * 128] = down

    def pack_copy(way, slot):
        return pltpu.make_async_remote_copy(
            src_ref=pack_out.at[way, slot],
            dst_ref=pack_in.at[way, slot],
            send_sem=pack_send.at[way, slot],
            recv_sem=pack_recv.at[way, slot],
            device_id=(above, below)[way],
            device_id_type=MESH,
        )

    def edge_copy(way):
        return pltpu.make_async_remote_copy(
            src_ref=edge_out.at[way],
            dst_ref=edge_in.at[way],
            send_sem=edge_send.at[way],
            recv_sem=edge_recv.at[way],
            device_id=(ahead, behind)[way],
            device_id_type=MESH,
        )

    def move_copy(way, k, chunk):
        patch = 5 + k if way == 0 else 4 - k
        slot = k if way == 0 else 4 - k
        part = pl.ds(chunk * CHUNK, CHUNK)
        return pltpu.make_async_remote_copy(
            src_ref=own_ref.at[patch, part],
            dst_ref=(left_ref, right_ref)[way].at[slot, part],
            send_sem=move_send.at[way, k, chunk],
            recv_sem=move_recv.at[way, k, chunk],
            device_id=(ahead, behind)[way],
            device_id_type=MESH,
        )

    def fix_copy(way):
        return pltpu.make_async_remote_copy(
            src_ref=fix_out.at[way],
            dst_ref=fix_in.at[way],
            send_sem=fix_send.at[way],
            recv_sem=fix_recv.at[way],
            device_id=(ahead, behind)[way],
            device_id_type=MESH,
        )

    def stage(slot):
        for field in range(2):
            for tile in range(TILES):
                values = coarse[field, slot, :, tile * 128 : (tile + 1) * 128]
                for i, rows in enumerate(split_pair(values)):
                    put_rows(staged.at[field, slot], 2 * tile + i - 1, rows)

    def stage_faces(slot):
        for tile in range(TILES):
            values = coarse[1, slot, :, tile * 128 : (tile + 1) * 128]
            for i, rows in enumerate(split_pair(values)):
                put_rows(outer.at[0], 2 * tile + i, rows)
                put_rows(outer.at[1], 2 * tile + i - 2, rows)
        faces[0:SPEC, :] = split_pair(coarse[0, slot, :, 0:128])[0]
        faces[PITCH : PITCH + SPEC, :] = split_pair(coarse[0, slot, :, COARSE - 128 : COARSE])[1]

    def spread(patch, closed=False):
        def dot(a, first, count):
            table = lane_mats[first * 128 : (first + count) * 128, :]
            return jnp.dot(a, table, preferred_element_type=jnp.float32)

        def keep(index, values, begins):
            for half in range(2):
                part = values[:, half * 128 : (half + 1) * 128]
                for begin in begins:
                    weights.at[index, half][pl.ds(begin, FLAT, stride=2), :] = part

        z = lane_iota(FLAT) % 8

        def across(field):
            low, high = staged[field, patch], staged[field, patch + 2]
            return jnp.where(z == 7, low, jnp.where(z == 0, high, 0.0)).astype(jnp.bfloat16)

        own = staged[1, patch + 1].astype(jnp.bfloat16)

        def beside(values):
            return jnp.concatenate([own, values], axis=1)

        both = (0, 1)
        keep(0, dot(own, 8, 1), both)
        for side in range(2):
            keep(1, dot(beside(outer[side].astype(jnp.bfloat16)), 0, 2), (side,))
        if closed:
            keep(2, dot(own, 2, 1), both)
        else:
            keep(2, dot(beside(sides[1].astype(jnp.bfloat16)), 2, 2), both)
            keep(4, dot(sides[0].astype(jnp.bfloat16), 6, 1), both)
        keep(3, dot(beside(across(1)), 4, 2), both)
        keep(5, dot(across(0), 7, 1), both)
        edge = dot(faces[...].astype(jnp.bfloat16), 8, 1)
        for half in range(2):
            face_rows[half] = edge[:, half * 128 : (half + 1) * 128]

    def diffuse(patch, chunk, closed=False):
        row = lax.broadcasted_iota(jnp.int32, (8, 128), 0)
        lanes = lax.broadcasted_iota(jnp.int32, (8, 128), 1)
        odd_x, odd_y, odd_z = row % 2 == 1, (lanes // EDGE) % 2 == 1, lanes % 2 == 1
        first_x, last_x = row == 0, row == 7
        first_y, last_y = lanes < EDGE, lanes >= 128 - EDGE
        face_z = (lanes % EDGE == 0) | (lanes % EDGE == EDGE - 1)

        def one(species):
            begin = pl.multiple_of(species * EDGE, EDGE)
            p = [
                [
                    cells[patch, species, 8 * h : 8 * h + 8, 128 * v : 128 * v + 128]
                    for v in range(2)
                ]
                for h in range(2)
            ]
            down_x = [[pltpu.roll(p[h][v], 1, 0) for v in range(2)] for h in range(2)]
            up_x = [[pltpu.roll(p[h][v], 7, 0) for v in range(2)] for h in range(2)]
            down_y = [[pltpu.roll(p[h][v], EDGE, 1) for v in range(2)] for h in range(2)]
            up_y = [[pltpu.roll(p[h][v], 128 - EDGE, 1) for v in range(2)] for h in range(2)]
            for h in range(2):
                for v in range(2):
                    own = p[h][v]

                    def load(index, h=h, v=v):
                        return weights[index, v, pl.ds(begin + 8 * h, 8), :]

                    outside = face_rows[v, pl.ds(species + PITCH * h, 1), :]
                    dx, ux, dy, uy = down_x[h][v], up_x[h][v], down_y[h][v], up_y[h][v]
                    dz, uz = pltpu.roll(own, 1, 1), pltpu.roll(own, 127, 1)
                    inner = jnp.where(odd_x, dx, ux) + jnp.where(odd_y, dy, uy)
                    inner = inner + jnp.where(odd_z, dz, uz)
                    far_x = jnp.where(odd_x, ux, dx)
                    far_y = jnp.where(odd_y, uy, dy)
                    if h == 0:
                        far_x = jnp.where(first_x, outside, jnp.where(last_x, up_x[1][v], far_x))
                    else:
                        far_x = jnp.where(last_x, outside, jnp.where(first_x, down_x[0][v], far_x))
                    y_outside = own if closed else load(4)
                    if v == 0:
                        far_y = jnp.where(first_y, y_outside, jnp.where(last_y, up_y[h][1], far_y))
                    else:
                        far_y = jnp.where(last_y, y_outside, jnp.where(first_y, down_y[h][0], far_y))
                    far_z = jnp.where(face_z, load(5), jnp.where(odd_z, uz, dz))
                    change = load(0) * (inner - 3.0 * own)
                    change = change + load(1) * (far_x - own)
                    change = change + load(2) * (far_y - own)
                    change = change + load(3) * (far_z - own)
                    own_ref[patch, species, 8 * h : 8 * h + 8, 128 * v : 128 * v + 128] = own + change

        def block(b, carry):
            for i in range(BLOCK):
                one(chunk * CHUNK + b * BLOCK + i)
            return carry

        lax.fori_loop(0, CHUNK // BLOCK, block, 0)

    lanes8 = lax.broadcasted_iota(jnp.int32, (8, 128), 1)
    group8 = lax.rem(lanes8 + EDGE, 128) // 32

    def fix(way, patch):
        low, high = lanes8 < EDGE, lanes8 >= 128 - EDGE
        packed = None
        for n in range(2 * CHUNK):
            species, h, j = n // 2, n % 2, n % 4
            terms = []
            for v in range(2):
                at = slice(species * EDGE + 8 * h, species * EDGE + 8 * h + 8)
                own = cells[patch, species, 8 * h : 8 * h + 8, 128 * v : 128 * v + 128]
                terms.append(weights[2, v, at, :] * (weights[4, v, at, :] - own))
            term = jnp.where(low, terms[0], jnp.where(high, terms[1], 0.0))
            if j == 0:
                packed = term
            else:
                packed = jnp.where(group8 == j, pltpu.roll(term, 32 * j, 1), packed)
            if j == 3:
                fix_out[way, 2 * (n - 3) : 2 * (n - 3) + 8, :] = packed

    def apply_fix(way, source, target, patch):
        for n in range(2 * CHUNK):
            species, h, j = n // 2, n % 2, n % 4
            term = source[way, 2 * (n - j) : 2 * (n - j) + 8, :]
            if j:
                term = pltpu.roll(term, 128 - 32 * j, 1)
            for v in range(2):
                lanes = slice(128 * v, 128 * v + 128)
                inside = lanes8 < EDGE if v == 0 else lanes8 >= 128 - EDGE
                old = target[patch, species, 8 * h : 8 * h + 8, lanes]
                target[patch, species, 8 * h : 8 * h + 8, lanes] = old + jnp.where(inside, term, 0.0)

    def smooth(way, k):
        patch = 5 + k if way == 0 else 4 - k
        slot = (k + 1) // 2
        base = 2 * lax.rem(k + 1, 2) + way
        stage_faces(patch + 1)
        for field in range(2):
            j = base * 2 + field
            back = 8 * j
            forth = lax.rem(128 - 8 * j, 128)
            for tile in range(TILES):
                part = slice(tile * 128, (tile + 1) * 128)
                low = pltpu.roll(pack_in[0, slot, :, part], back, 1)
                high = pltpu.roll(pack_in[1, slot, :, part], forth, 1)
                values = jnp.where(row_of == 7, low, jnp.where(row_of == 0, high, 0.0))
                for i, rows in enumerate(split_pair(values)):
                    put_rows(sides.at[field], 2 * tile + i - 1, rows)
        spread(patch)

        @pl.when(k > 0)
        def _():
            load_cells(patch).wait()
            diffuse(patch, 0)
            move_copy(way, k, 0).start()

        for chunk in range(1, CHUNKS):
            diffuse(patch, chunk)
            move_copy(way, k, chunk).start()

        @pl.when(k == 0)
        def _():
            fix(way, patch)
            fix_copy(way).start()

    for field in range(2):
        load_coarse(field, 0, *parts[0]).wait()
    pack(0, (5, 4), 2)
    pl.semaphore_wait(barrier, 4)
    for way in range(2):
        pack_copy(way, 0).start()
    for slot in (5, 6, 7, 4):
        stage(slot)
    load_table().wait()
    for way, patch in ((0, 5), (1, 4)):
        stage_faces(patch + 1)
        spread(patch, closed=True)
        load_cells(patch).wait()
        diffuse(patch, 0, closed=True)
        move_copy(way, 0, 0).start()
    for part in (1, 2):
        for field in range(2):
            load_coarse(field, part, *parts[part]).wait()
    pack(1, (6, 3, 7, 2), 0)
    for way in range(2):
        pack_copy(way, 1).start()

    def step(k, carry):
        @pl.when(k == 0)
        def _():
            for way in range(2):
                pack_copy(way, 0).wait_recv()

        @pl.when(k == 1)
        def _():
            for way in range(2):
                pack_copy(way, 1).wait_recv()

            for way in range(2):
                move_copy(way, 0, 0).wait_send()
                apply_fix(way, fix_out, own_ref, 5 - way)

        @pl.when(k == 3)
        def _():
            for way in range(2):
                pack_copy(way, 2).wait_recv()
                move_copy(way, 0, 0).wait_recv()
                fix_copy(way).wait_recv()
                apply_fix(way, fix_in, (left_ref, right_ref)[way], 4 * way)

        @pl.when(k == 4)
        def _():
            for way in range(2):
                edge_copy(way).wait_recv()
            for field in range(2):
                for tile in range(TILES):
                    part = slice(tile * 128, (tile + 1) * 128)
                    low = pltpu.roll(edge_in[0, field], (7 - tile) % 128, 1)
                    high = pltpu.roll(edge_in[1, field], (128 - tile) % 128, 1)
                    coarse[field, 0, :, part] = low
                    coarse[field, 11, :, part] = high

        @pl.when(k > 0)
        def _():
            stage(7 + k)
            stage(4 - k)

        smooth(0, k)
        smooth(1, k)

        @pl.when(k == 0)
        def _():
            pack(2, (8, 1, 9, 0), 0)
            for field in range(2):
                up = jnp.zeros((SPEC, 128), jnp.float32)
                down = jnp.zeros((SPEC, 128), jnp.float32)
                for tile in range(TILES):
                    part = slice(tile * 128, (tile + 1) * 128)
                    last = coarse[field, PATCHES, :, part]
                    first = coarse[field, 1, :, part]
                    up = jnp.where(lane % 8 == tile, pltpu.roll(last, (128 + tile - 7) % 128, 1), up)
                    down = jnp.where(lane % 8 == tile, pltpu.roll(first, tile, 1), down)
                edge_out[0, field] = up
                edge_out[1, field] = down
            for way in range(2):
                pack_copy(way, 2).start()
                edge_copy(way).start()

        return carry

    lax.fori_loop(0, HALF, step, 0)

    for way in range(2):
        for slot in range(3):
            pack_copy(way, slot).wait_send()
        edge_copy(way).wait_send()
        for k in range(HALF):
            for chunk in range(1 if k == 0 else 0, CHUNKS):
                move_copy(way, k, chunk).wait()
        fix_copy(way).wait_send()


def place_kernel(shift_ref, own_ref, left_ref, right_ref, out_ref, zeros, sem):
    curve = lax.axis_index("curve")
    here = shift_ref[0, curve]
    before = jnp.where(curve > 0, shift_ref[0, jnp.maximum(curve - 1, 0)], 0)
    count = PATCHES + here - before
    zeros[...] = jnp.zeros_like(zeros)
    for slot in range(2 * PATCHES):
        position = before + slot
        used = slot < count
        target = out_ref.at[slot]

        def put(source):
            pltpu.make_async_copy(source, target, sem).start()

        @pl.when(used & (position < 0))
        def _():
            put(left_ref.at[jnp.clip(position + HALF, 0, HALF - 1)])

        @pl.when(used & (position >= PATCHES))
        def _():
            put(right_ref.at[jnp.clip(position - PATCHES, 0, HALF - 1)])

        @pl.when(used & (position >= 0) & (position < PATCHES))
        def _():
            put(own_ref.at[jnp.clip(position, 0, PATCHES - 1)])

        @pl.when(jnp.logical_not(used))
        def _():
            put(zeros)

    pltpu.make_async_copy(out_ref, out_ref, sem).wait()


def shards(state, coarse_state, coarse_kappa, bound_shift):
    f32, bf16 = jnp.float32, jnp.bfloat16
    patch = (SPEC, EDGE, LANES)
    hbm = pl.BlockSpec(memory_space=pltpu.HBM)
    vmem = pl.BlockSpec(memory_space=pltpu.VMEM)
    lane_table = jnp.asarray(lane_tables(), bf16)
    operands = (state, coarse_state, coarse_kappa, lane_table)
    own, left, right = pl.pallas_call(
        exchange_kernel,
        name="exchange",
        out_shape=[
            jax.ShapeDtypeStruct((count,) + patch, f32) for count in (PATCHES, HALF, HALF)
        ],
        in_specs=[hbm] * 4,
        out_specs=[vmem] * 3,
        scratch_shapes=[
            pltpu.VMEM((PATCHES,) + patch, f32),
            pltpu.VMEM((2, PATCHES + 2, SPEC, COARSE), f32),
            pltpu.VMEM(lane_table.shape, bf16),
            pltpu.VMEM((2, PATCHES + 2, FLAT, 128), f32),
            pltpu.VMEM((2, FLAT, 128), f32),
            pltpu.VMEM((2, FLAT, 128), f32),
            pltpu.VMEM((2 * PITCH, 128), f32),
            pltpu.VMEM((2, 2 * PITCH, 128), f32),
            pltpu.VMEM((2, 3, SPEC, COARSE), f32),
            pltpu.VMEM((2, 3, SPEC, COARSE), f32),
            pltpu.VMEM((2, 2, SPEC, 128), f32),
            pltpu.VMEM((2, 2, SPEC, 128), f32),
            pltpu.VMEM((6, 2, 2 * FLAT, 128), f32),
            pltpu.VMEM((2, 4 * CHUNK, 128), f32),
            pltpu.VMEM((2, 4 * CHUNK, 128), f32),
            pltpu.SemaphoreType.DMA((PATCHES,)),
            pltpu.SemaphoreType.DMA((2, 3)),
            pltpu.SemaphoreType.DMA,
            pltpu.SemaphoreType.DMA((2, 3)),
            pltpu.SemaphoreType.DMA((2, 3)),
            pltpu.SemaphoreType.DMA((2,)),
            pltpu.SemaphoreType.DMA((2,)),
            pltpu.SemaphoreType.DMA((2, HALF, CHUNKS)),
            pltpu.SemaphoreType.DMA((2, HALF, CHUNKS)),
            pltpu.SemaphoreType.DMA((2,)),
            pltpu.SemaphoreType.DMA((2,)),
        ],
        compiler_params=pltpu.CompilerParams(
            collective_id=0, has_side_effects=True, vmem_limit_bytes=36 << 20
        ),
        cost_estimate=pl.CostEstimate(flops=8 << 30, bytes_accessed=12 << 20, transcendentals=0),
    )(*(pltpu.with_memory_space_constraint(v, pltpu.HBM) for v in operands))
    return pl.pallas_call(
        place_kernel,
        name="place",
        out_shape=jax.ShapeDtypeStruct((2 * PATCHES,) + patch, f32),
        in_specs=[pl.BlockSpec(memory_space=pltpu.SMEM)] + [vmem] * 3,
        out_specs=hbm,
        scratch_shapes=[pltpu.VMEM(patch, f32), pltpu.SemaphoreType.DMA],
        compiler_params=pltpu.CompilerParams(vmem_limit_bytes=16 << 20),
        cost_estimate=pl.CostEstimate(flops=0, bytes_accessed=7 << 20, transcendentals=0),
    )(bound_shift, own, left, right)


def solution(mesh):
    in_specs = (
        P(("curve", "group"), None, None, None),
        P(("curve", "group"), None, None),
        P(("curve", "group"), None, None),
        P("group", None),
    )
    out_specs = P(("curve", "group"), None, None, None)
    return jax.shard_map(shards, mesh=mesh, in_specs=in_specs, out_specs=out_specs, check_vma=False)
```

```python
import jax
import jax.numpy as jnp
import numpy as np
from jax import lax
from jax.experimental import pallas as pl
from jax.experimental.pallas import tpu as pltpu
from jax.sharding import PartitionSpec as P

MESH = pl.DeviceIdType.MESH
SPEC = 20
EDGE = 16
LANES = EDGE * EDGE
PATCHES = 10
HALF = 5
COARSE = 640
PITCH = 24
TILES = COARSE // 128
CHUNK = 10
CHUNKS = SPEC // CHUNK
BLOCK = 2
EARLY = 2
FLAT = SPEC * 8


def lane_tables():
    half = np.zeros((64, LANES), np.float32)
    y_own, y_side, y_face = np.zeros_like(half), np.zeros_like(half), np.zeros_like(half)
    z_own, z_side, z_face = np.zeros_like(half), np.zeros_like(half), np.zeros_like(half)
    for r in range(EDGE):
        for q in range(EDGE):
            lane, cy, cz = r * EDGE + q, r // 2, q // 2
            here = cy * 8 + cz
            half[here, lane] = 0.5
            y_own[here, lane] += 0.5
            z_own[here, lane] += 0.5
            near = r + 1 if r % 2 else r - 1
            if near < 0:
                y_side[56 + cz, lane], y_face[56 + cz, lane] = 0.5, 1.0
            elif near >= EDGE:
                y_side[cz, lane], y_face[cz, lane] = 0.5, 1.0
            else:
                y_own[near // 2 * 8 + cz, lane] += 0.5
            near = q + 1 if q % 2 else q - 1
            if near < 0:
                z_side[cy * 8 + 7, lane], z_face[cy * 8 + 7, lane] = 0.5, 1.0
            elif near >= EDGE:
                z_side[cy * 8, lane], z_face[cy * 8, lane] = 0.5, 1.0
            else:
                z_own[cy * 8 + near // 2, lane] += 0.5
    parts = [half, half, y_own, y_side, z_own, z_side, y_face, z_face, 2.0 * half]
    return np.concatenate([np.concatenate([part, part]) for part in parts])


def lane_iota(rows):
    return lax.broadcasted_iota(jnp.int32, (rows, 128), 1)


def split_pair(values):
    lane = lane_iota(SPEC)
    high = values.astype(jnp.bfloat16).astype(jnp.float32)
    rest = values - high
    even = jnp.where(lane < 64, high, pltpu.roll(rest, 64, 1))
    odd = jnp.where(lane < 64, pltpu.roll(high, 64, 1), rest)
    return even, odd


def put_rows(target, place, values):
    if 0 <= place < 8:
        target[pl.ds(place, SPEC, stride=8), :] = values


def exchange_kernel(
    state_ref,
    coarse_state_ref,
    coarse_kappa_ref,
    lanes_ref,
    own_ref,
    moved_ref,
    cells,
    coarse,
    lane_mats,
    staged,
    outer,
    sides,
    faces,
    face_rows,
    pack_out,
    pack_in,
    edge_out,
    edge_in,
    weights,
    fix_out,
    fix_in,
    cell_sem,
    coarse_sem,
    table_sem,
    pack_send,
    pack_recv,
    edge_send,
    edge_recv,
    move_send,
    move_recv,
    fix_send,
    fix_recv,
):
    curve = lax.axis_index("curve")
    group = lax.axis_index("group")
    n_curve = lax.axis_size("curve")
    n_group = lax.axis_size("group")
    ahead = (lax.rem(curve + 1, n_curve), group)
    behind = (lax.rem(curve + n_curve - 1, n_curve), group)
    above = (curve, lax.rem(group + 1, n_group))
    below = (curve, lax.rem(group + n_group - 1, n_group))

    def load_coarse(field, part, begin, count):
        source = (coarse_state_ref, coarse_kappa_ref)[field]
        return pltpu.make_async_copy(
            source.at[pl.ds(begin, count)],
            coarse.at[field, pl.ds(begin + 1, count)],
            coarse_sem.at[field, part],
        )

    def load_cells(patch):
        return pltpu.make_async_copy(state_ref.at[patch], cells.at[patch], cell_sem.at[patch])

    def load_table():
        return pltpu.make_async_copy(lanes_ref, lane_mats, table_sem)

    parts = ((3, 4), (0, 3), (7, 3))
    for field in range(2):
        load_coarse(field, 0, *parts[0]).start()
    load_table().start()
    for patch in (4, 5):
        load_cells(patch).start()
    for part in (1, 2):
        for field in range(2):
            load_coarse(field, part, *parts[part]).start()
    for patch in (3, 6, 2, 7, 1, 8, 0, 9):
        load_cells(patch).start()

    barrier = pltpu.get_barrier_semaphore()
    for device in (above, below, ahead, behind):
        pl.semaphore_signal(barrier, inc=1, device_id=device, device_id_type=MESH)

    faces[...] = jnp.zeros_like(faces)

    lane = lane_iota(SPEC)
    row_of = (lane % 64) // 8

    def pack(slot, patches, first):
        for tile in range(TILES):
            up = jnp.zeros((SPEC, 128), jnp.float32)
            down = jnp.zeros((SPEC, 128), jnp.float32)
            for place, patch in enumerate(patches):
                for field in range(2):
                    j = (first + place) * 2 + field
                    values = coarse[field, patch + 1, :, tile * 128 : (tile + 1) * 128]
                    up = jnp.where(row_of == 7 - j, pltpu.roll(values, (128 - 8 * j) % 128, 1), up)
                    down = jnp.where(row_of == j, pltpu.roll(values, 8 * j, 1), down)
            pack_out[0, slot, :, tile * 128 : (tile + 1) * 128] = up
            pack_out[1, slot, :, tile * 128 : (tile + 1) * 128] = down

    def pack_copy(way, slot):
        return pltpu.make_async_remote_copy(
            src_ref=pack_out.at[way, slot],
            dst_ref=pack_in.at[way, slot],
            send_sem=pack_send.at[way, slot],
            recv_sem=pack_recv.at[way, slot],
            device_id=(above, below)[way],
            device_id_type=MESH,
        )

    def toward(way):
        return (jnp.where(way == 0, ahead[0], behind[0]), group)

    def leaving(way, k):
        return jnp.where(way == 0, HALF + k, HALF - 1 - k)

    def edge_copy(way):
        return pltpu.make_async_remote_copy(
            src_ref=edge_out.at[way],
            dst_ref=edge_in.at[way],
            send_sem=edge_send.at[way],
            recv_sem=edge_recv.at[way],
            device_id=(ahead, behind)[way],
            device_id_type=MESH,
        )

    def move_copy(way, k, chunk):
        part = pl.ds(chunk * CHUNK, CHUNK)
        return pltpu.make_async_remote_copy(
            src_ref=own_ref.at[leaving(way, k), part],
            dst_ref=moved_ref.at[way, jnp.where(way == 0, k, HALF - 1 - k), part],
            send_sem=move_send.at[way, k, chunk],
            recv_sem=move_recv.at[way, k, chunk],
            device_id=toward(way),
            device_id_type=MESH,
        )

    def sends(way):
        return jnp.where(way == 0, curve < n_curve - 1, curve > 0)

    def gets(way):
        return jnp.where(way == 0, curve > 0, curve < n_curve - 1)

    def send_move(way, k, chunk):
        @pl.when(sends(way))
        def _():
            move_copy(way, k, chunk).start()

    def fix_copy(way):
        return pltpu.make_async_remote_copy(
            src_ref=fix_out.at[way],
            dst_ref=fix_in.at[way],
            send_sem=fix_send.at[way],
            recv_sem=fix_recv.at[way],
            device_id=toward(way),
            device_id_type=MESH,
        )

    def stage(slot):
        for field in range(2):
            for tile in range(TILES):
                values = coarse[field, slot, :, tile * 128 : (tile + 1) * 128]
                for i, rows in enumerate(split_pair(values)):
                    put_rows(staged.at[field, slot], 2 * tile + i - 1, rows)

    def stage_faces(slot):
        for tile in range(TILES):
            values = coarse[1, slot, :, tile * 128 : (tile + 1) * 128]
            for i, rows in enumerate(split_pair(values)):
                put_rows(outer.at[0], 2 * tile + i, rows)
                put_rows(outer.at[1], 2 * tile + i - 2, rows)
        faces[0:SPEC, :] = split_pair(coarse[0, slot, :, 0:128])[0]
        faces[PITCH : PITCH + SPEC, :] = split_pair(coarse[0, slot, :, COARSE - 128 : COARSE])[1]

    def dot(a, first, count):
        table = lane_mats[first * 128 : (first + count) * 128, :]
        return jnp.dot(a, table, preferred_element_type=jnp.float32)

    def keep(way, index, values, begins=(0, 1)):
        for half in range(2):
            part = values[:, half * 128 : (half + 1) * 128]
            for begin in begins:
                weights.at[way, index, half][pl.ds(begin, FLAT, stride=2), :] = part

    def spread(way, patch):
        z = lane_iota(FLAT) % 8

        def across(field):
            low, high = staged[field, patch], staged[field, patch + 2]
            return jnp.where(z == 7, low, jnp.where(z == 0, high, 0.0)).astype(jnp.bfloat16)

        own = staged[1, patch + 1].astype(jnp.bfloat16)

        def beside(values):
            return jnp.concatenate([own, values], axis=1)

        keep(way, 0, dot(own, 8, 1))
        for side in range(2):
            keep(way, 1, dot(beside(outer[side].astype(jnp.bfloat16)), 0, 2), (side,))
        keep(way, 3, dot(beside(across(1)), 4, 2))
        keep(way, 5, dot(across(0), 7, 1))
        edge = dot(faces[...].astype(jnp.bfloat16), 8, 1)
        for half in range(2):
            face_rows[way, half] = edge[:, half * 128 : (half + 1) * 128]

    def spread_y(way, patch, closed):
        own = staged[1, patch + 1].astype(jnp.bfloat16)
        if closed:
            keep(way, 2, dot(own, 2, 1))
        else:
            beside = jnp.concatenate([own, sides[1].astype(jnp.bfloat16)], axis=1)
            keep(way, 2, dot(beside, 2, 2))
            keep(way, 4, dot(sides[0].astype(jnp.bfloat16), 6, 1))

    def diffuse(way, patch, chunk, closed=False):
        row = lax.broadcasted_iota(jnp.int32, (8, 128), 0)
        lanes = lax.broadcasted_iota(jnp.int32, (8, 128), 1)
        odd_x, odd_y, odd_z = row % 2 == 1, (lanes // EDGE) % 2 == 1, lanes % 2 == 1
        first_x, last_x = row == 0, row == 7
        first_y, last_y = lanes < EDGE, lanes >= 128 - EDGE
        face_z = (lanes % EDGE == 0) | (lanes % EDGE == EDGE - 1)

        def one(species):
            begin = pl.multiple_of(species * EDGE, EDGE)
            p = [
                [
                    cells[patch, species, 8 * h : 8 * h + 8, 128 * v : 128 * v + 128]
                    for v in range(2)
                ]
                for h in range(2)
            ]
            down_x = [[pltpu.roll(p[h][v], 1, 0) for v in range(2)] for h in range(2)]
            up_x = [[pltpu.roll(p[h][v], 7, 0) for v in range(2)] for h in range(2)]
            down_y = [[pltpu.roll(p[h][v], EDGE, 1) for v in range(2)] for h in range(2)]
            up_y = [[pltpu.roll(p[h][v], 128 - EDGE, 1) for v in range(2)] for h in range(2)]
            for h in range(2):
                for v in range(2):
                    own = p[h][v]

                    def load(index, h=h, v=v):
                        return weights[way, index, v, pl.ds(begin + 8 * h, 8), :]

                    outside = face_rows[way, v, pl.ds(species + PITCH * h, 1), :]
                    dx, ux, dy, uy = down_x[h][v], up_x[h][v], down_y[h][v], up_y[h][v]
                    dz, uz = pltpu.roll(own, 1, 1), pltpu.roll(own, 127, 1)
                    inner = jnp.where(odd_x, dx, ux) + jnp.where(odd_y, dy, uy)
                    inner = inner + jnp.where(odd_z, dz, uz)
                    far_x = jnp.where(odd_x, ux, dx)
                    far_y = jnp.where(odd_y, uy, dy)
                    if h == 0:
                        far_x = jnp.where(first_x, outside, jnp.where(last_x, up_x[1][v], far_x))
                    else:
                        far_x = jnp.where(last_x, outside, jnp.where(first_x, down_x[0][v], far_x))
                    y_outside = own if closed else load(4)
                    if v == 0:
                        far_y = jnp.where(first_y, y_outside, jnp.where(last_y, up_y[h][1], far_y))
                    else:
                        far_y = jnp.where(last_y, y_outside, jnp.where(first_y, down_y[h][0], far_y))
                    far_z = jnp.where(face_z, load(5), jnp.where(odd_z, uz, dz))
                    change = load(0) * (inner - 3.0 * own)
                    change = change + load(1) * (far_x - own)
                    change = change + load(2) * (far_y - own)
                    change = change + load(3) * (far_z - own)
                    own_ref[patch, species, 8 * h : 8 * h + 8, 128 * v : 128 * v + 128] = own + change

        def block(b, carry):
            for i in range(BLOCK):
                one(chunk * CHUNK + b * BLOCK + i)
            return carry

        lax.fori_loop(0, CHUNK // BLOCK, block, 0)

    lanes8 = lax.broadcasted_iota(jnp.int32, (8, 128), 1)
    group8 = lax.rem(lanes8 + EDGE, 128) // 32

    def fix(way, patch):
        low, high = lanes8 < EDGE, lanes8 >= 128 - EDGE
        packed = None
        for n in range(2 * EARLY * CHUNK):
            species, h, j = n // 2, n % 2, n % 4
            terms = []
            for v in range(2):
                at = slice(species * EDGE + 8 * h, species * EDGE + 8 * h + 8)
                own = cells[patch, species, 8 * h : 8 * h + 8, 128 * v : 128 * v + 128]
                terms.append(weights[way, 2, v, at, :] * (weights[way, 4, v, at, :] - own))
            term = jnp.where(low, terms[0], jnp.where(high, terms[1], 0.0))
            if j == 0:
                packed = term
            else:
                packed = jnp.where(group8 == j, pltpu.roll(term, 32 * j, 1), packed)
            if j == 3:
                fix_out[way, 2 * (n - 3) : 2 * (n - 3) + 8, :] = packed

    def apply_fix(way, source, target, patch):
        for n in range(2 * EARLY * CHUNK):
            species, h, j = n // 2, n % 2, n % 4
            term = source[way, 2 * (n - j) : 2 * (n - j) + 8, :]
            if j:
                term = pltpu.roll(term, 128 - 32 * j, 1)
            for v in range(2):
                lanes = slice(128 * v, 128 * v + 128)
                inside = lanes8 < EDGE if v == 0 else lanes8 >= 128 - EDGE
                old = target[patch, species, 8 * h : 8 * h + 8, lanes]
                target[patch, species, 8 * h : 8 * h + 8, lanes] = old + jnp.where(inside, term, 0.0)

    def smooth(way, k):
        patch = leaving(way, k)
        slot = (k + 1) // 2
        base = 2 * lax.rem(k + 1, 2) + way

        @pl.when(k > 0)
        def _():
            stage_faces(patch + 1)
            spread(way, patch)

        for field in range(2):
            j = base * 2 + field
            back = 8 * j
            forth = lax.rem(128 - 8 * j, 128)
            for tile in range(TILES):
                part = slice(tile * 128, (tile + 1) * 128)
                low = pltpu.roll(pack_in[0, slot, :, part], back, 1)
                high = pltpu.roll(pack_in[1, slot, :, part], forth, 1)
                values = jnp.where(row_of == 7, low, jnp.where(row_of == 0, high, 0.0))
                for i, rows in enumerate(split_pair(values)):
                    put_rows(sides.at[field], 2 * tile + i - 1, rows)
        spread_y(way, patch, False)

        @pl.when(k > 0)
        def _():
            load_cells(patch).wait()
            for chunk in range(EARLY):
                diffuse(way, patch, chunk)
                send_move(way, k, chunk)

        for chunk in range(EARLY, CHUNKS):
            diffuse(way, patch, chunk)
            send_move(way, k, chunk)

        @pl.when(k == 0)
        def _():
            fix(way, patch)

            @pl.when(sends(way))
            def _():
                fix_copy(way).start()

    for field in range(2):
        load_coarse(field, 0, *parts[0]).wait()
    for slot in (5, 6, 7, 4):
        stage(slot)
    load_table().wait()
    for turn in range(2):
        way = 1 - turn
        patch = leaving(way, 0)
        stage_faces(patch + 1)
        spread(way, patch)
        spread_y(way, patch, True)
        load_cells(patch).wait()
        diffuse(way, patch, 0, closed=True)
        if turn == 0:
            pl.semaphore_wait(barrier, 4)
        send_move(way, 0, 0)
        if turn == 0:
            pack(0, (5, 4), 2)
            for side in range(2):
                pack_copy(side, 0).start()
    for part in (1, 2):
        for field in range(2):
            load_coarse(field, part, *parts[part]).wait()
    pack(1, (6, 3, 7, 2), 0)
    for way in range(2):
        pack_copy(way, 1).start()

    for chunk in range(1, EARLY):
        for turn in range(2):
            way = 1 - turn
            diffuse(way, leaving(way, 0), chunk, closed=True)
            send_move(way, 0, chunk)

    def step(m, carry):
        k = m // 2
        for slot, turn in ((0, 0), (1, 2), (2, 6)):

            @pl.when(m == turn)
            def _(slot=slot):
                for way in range(2):
                    pack_copy(way, slot).wait_recv()

        @pl.when(m == 6)
        def _():
            for way in range(2):

                @pl.when(sends(way))
                def _(way=way):
                    for chunk in range(EARLY):
                        move_copy(way, 0, chunk).wait_send()

                apply_fix(way, fix_out, own_ref, 5 - way)

                @pl.when(gets(way))
                def _(way=way):
                    for chunk in range(EARLY):
                        move_copy(way, 0, chunk).wait_recv()
                    fix_copy(way).wait_recv()
                    apply_fix(way, fix_in, moved_ref.at[way], 4 * way)

        @pl.when(m == 8)
        def _():
            for way in range(2):
                edge_copy(way).wait_recv()
            for field in range(2):
                for tile in range(TILES):
                    part = slice(tile * 128, (tile + 1) * 128)
                    low = pltpu.roll(edge_in[0, field], (7 - tile) % 128, 1)
                    high = pltpu.roll(edge_in[1, field], (128 - tile) % 128, 1)
                    coarse[field, 0, :, part] = low
                    coarse[field, 11, :, part] = high

        @pl.when((m > 1) & (lax.rem(m, 2) == 0))
        def _():
            stage(7 + k)
            stage(4 - k)

        smooth(1 - lax.rem(m, 2), k)

        @pl.when(m == 1)
        def _():
            pack(2, (8, 1, 9, 0), 0)
            for field in range(2):
                up = jnp.zeros((SPEC, 128), jnp.float32)
                down = jnp.zeros((SPEC, 128), jnp.float32)
                for tile in range(TILES):
                    part = slice(tile * 128, (tile + 1) * 128)
                    last = coarse[field, PATCHES, :, part]
                    first = coarse[field, 1, :, part]
                    up = jnp.where(lane % 8 == tile, pltpu.roll(last, (128 + tile - 7) % 128, 1), up)
                    down = jnp.where(lane % 8 == tile, pltpu.roll(first, tile, 1), down)
                edge_out[0, field] = up
                edge_out[1, field] = down
            for way in range(2):
                pack_copy(way, 2).start()
                edge_copy(way).start()

        return carry

    lax.fori_loop(0, 2 * HALF, step, 0)

    for way in range(2):
        for slot in range(3):
            pack_copy(way, slot).wait_send()
        edge_copy(way).wait_send()

        @pl.when(sends(way))
        def _(way=way):
            fix_copy(way).wait_send()
            for k in range(HALF):
                for chunk in range(EARLY if k == 0 else 0, CHUNKS):
                    move_copy(way, k, chunk).wait_send()

        @pl.when(gets(way))
        def _(way=way):
            for k in range(HALF):
                for chunk in range(EARLY if k == 0 else 0, CHUNKS):
                    move_copy(way, k, chunk).wait_recv()


def place_kernel(shift_ref, own_ref, moved_ref, out_ref, zeros, sem):
    curve = lax.axis_index("curve")
    here = shift_ref[0, curve]
    before = jnp.where(curve > 0, shift_ref[0, jnp.maximum(curve - 1, 0)], 0)
    count = PATCHES + here - before
    zeros[...] = jnp.zeros_like(zeros)
    for slot in range(2 * PATCHES):
        position = before + slot
        used = slot < count
        target = out_ref.at[slot]

        def put(source):
            pltpu.make_async_copy(source, target, sem).start()

        @pl.when(used & (position < 0))
        def _():
            put(moved_ref.at[0, jnp.clip(position + HALF, 0, HALF - 1)])

        @pl.when(used & (position >= PATCHES))
        def _():
            put(moved_ref.at[1, jnp.clip(position - PATCHES, 0, HALF - 1)])

        @pl.when(used & (position >= 0) & (position < PATCHES))
        def _():
            put(own_ref.at[jnp.clip(position, 0, PATCHES - 1)])

        @pl.when(jnp.logical_not(used))
        def _():
            put(zeros)

    pltpu.make_async_copy(out_ref, out_ref, sem).wait()


def shards(state, coarse_state, coarse_kappa, bound_shift):
    f32, bf16 = jnp.float32, jnp.bfloat16
    patch = (SPEC, EDGE, LANES)
    hbm = pl.BlockSpec(memory_space=pltpu.HBM)
    vmem = pl.BlockSpec(memory_space=pltpu.VMEM)
    lane_table = jnp.asarray(lane_tables(), bf16)
    operands = (state, coarse_state, coarse_kappa, lane_table)
    own, moved = pl.pallas_call(
        exchange_kernel,
        name="exchange",
        out_shape=[
            jax.ShapeDtypeStruct((PATCHES,) + patch, f32),
            jax.ShapeDtypeStruct((2, HALF) + patch, f32),
        ],
        in_specs=[hbm] * 4,
        out_specs=[vmem] * 2,
        scratch_shapes=[
            pltpu.VMEM((PATCHES,) + patch, f32),
            pltpu.VMEM((2, PATCHES + 2, SPEC, COARSE), f32),
            pltpu.VMEM(lane_table.shape, bf16),
            pltpu.VMEM((2, PATCHES + 2, FLAT, 128), f32),
            pltpu.VMEM((2, FLAT, 128), f32),
            pltpu.VMEM((2, FLAT, 128), f32),
            pltpu.VMEM((2 * PITCH, 128), f32),
            pltpu.VMEM((2, 2, 2 * PITCH, 128), f32),
            pltpu.VMEM((2, 3, SPEC, COARSE), f32),
            pltpu.VMEM((2, 3, SPEC, COARSE), f32),
            pltpu.VMEM((2, 2, SPEC, 128), f32),
            pltpu.VMEM((2, 2, SPEC, 128), f32),
            pltpu.VMEM((2, 6, 2, 2 * FLAT, 128), f32),
            pltpu.VMEM((2, 4 * EARLY * CHUNK, 128), f32),
            pltpu.VMEM((2, 4 * EARLY * CHUNK, 128), f32),
            pltpu.SemaphoreType.DMA((PATCHES,)),
            pltpu.SemaphoreType.DMA((2, 3)),
            pltpu.SemaphoreType.DMA,
            pltpu.SemaphoreType.DMA((2, 3)),
            pltpu.SemaphoreType.DMA((2, 3)),
            pltpu.SemaphoreType.DMA((2,)),
            pltpu.SemaphoreType.DMA((2,)),
            pltpu.SemaphoreType.DMA((2, HALF, CHUNKS)),
            pltpu.SemaphoreType.DMA((2, HALF, CHUNKS)),
            pltpu.SemaphoreType.DMA((2,)),
            pltpu.SemaphoreType.DMA((2,)),
        ],
        compiler_params=pltpu.CompilerParams(
            collective_id=0, has_side_effects=True, vmem_limit_bytes=36 << 20
        ),
        cost_estimate=pl.CostEstimate(flops=8 << 30, bytes_accessed=12 << 20, transcendentals=0),
    )(*(pltpu.with_memory_space_constraint(v, pltpu.HBM) for v in operands))
    return pl.pallas_call(
        place_kernel,
        name="place",
        out_shape=jax.ShapeDtypeStruct((2 * PATCHES,) + patch, f32),
        in_specs=[pl.BlockSpec(memory_space=pltpu.SMEM)] + [vmem] * 2,
        out_specs=hbm,
        scratch_shapes=[pltpu.VMEM(patch, f32), pltpu.SemaphoreType.DMA],
        compiler_params=pltpu.CompilerParams(vmem_limit_bytes=16 << 20),
        cost_estimate=pl.CostEstimate(flops=0, bytes_accessed=7 << 20, transcendentals=0),
    )(bound_shift, own, moved)


def solution(mesh):
    in_specs = (
        P(("curve", "group"), None, None, None),
        P(("curve", "group"), None, None),
        P(("curve", "group"), None, None),
        P("group", None),
    )
    out_specs = P(("curve", "group"), None, None, None)
    return jax.shard_map(shards, mesh=mesh, in_specs=in_specs, out_specs=out_specs, check_vma=False)
```

```python
import jax
import jax.numpy as jnp
import numpy as np
from jax import lax
from jax.experimental import pallas as pl
from jax.experimental.pallas import tpu as pltpu
from jax.sharding import PartitionSpec as P

MESH = pl.DeviceIdType.MESH
SPEC = 20
EDGE = 16
LANES = EDGE * EDGE
PATCHES = 10
HALF = 5
COARSE = 640
PITCH = 24
TILES = COARSE // 128
CHUNK = 10
CHUNKS = SPEC // CHUNK
BLOCK = 2
EARLY = 2
FLAT = SPEC * 8


def lane_tables():
    half = np.zeros((64, LANES), np.float32)
    y_own, y_side, y_face = np.zeros_like(half), np.zeros_like(half), np.zeros_like(half)
    z_own, z_side, z_face = np.zeros_like(half), np.zeros_like(half), np.zeros_like(half)
    for r in range(EDGE):
        for q in range(EDGE):
            lane, cy, cz = r * EDGE + q, r // 2, q // 2
            here = cy * 8 + cz
            half[here, lane] = 0.5
            y_own[here, lane] += 0.5
            z_own[here, lane] += 0.5
            near = r + 1 if r % 2 else r - 1
            if near < 0:
                y_side[56 + cz, lane], y_face[56 + cz, lane] = 0.5, 1.0
            elif near >= EDGE:
                y_side[cz, lane], y_face[cz, lane] = 0.5, 1.0
            else:
                y_own[near // 2 * 8 + cz, lane] += 0.5
            near = q + 1 if q % 2 else q - 1
            if near < 0:
                z_side[cy * 8 + 7, lane], z_face[cy * 8 + 7, lane] = 0.5, 1.0
            elif near >= EDGE:
                z_side[cy * 8, lane], z_face[cy * 8, lane] = 0.5, 1.0
            else:
                z_own[cy * 8 + near // 2, lane] += 0.5
    parts = [half, half, y_own, y_side, z_own, z_side, y_face, z_face, 2.0 * half]
    return np.concatenate([np.concatenate([part, part]) for part in parts])


def lane_iota(rows):
    return lax.broadcasted_iota(jnp.int32, (rows, 128), 1)


def split_pair(values):
    lane = lane_iota(SPEC)
    high = values.astype(jnp.bfloat16).astype(jnp.float32)
    rest = values - high
    even = jnp.where(lane < 64, high, pltpu.roll(rest, 64, 1))
    odd = jnp.where(lane < 64, pltpu.roll(high, 64, 1), rest)
    return even, odd


def put_rows(target, place, values):
    if 0 <= place < 8:
        target[pl.ds(place, SPEC, stride=8), :] = values


def exchange_kernel(
    state_ref,
    coarse_state_ref,
    coarse_kappa_ref,
    lanes_ref,
    own_ref,
    moved_ref,
    cells,
    coarse,
    lane_mats,
    staged,
    outer,
    sides,
    faces,
    face_rows,
    pack_out,
    pack_in,
    edge_out,
    edge_in,
    weights,
    fix_out,
    fix_in,
    cell_sem,
    coarse_sem,
    table_sem,
    pack_send,
    pack_recv,
    edge_send,
    edge_recv,
    move_send,
    move_recv,
    fix_send,
    fix_recv,
):
    curve = lax.axis_index("curve")
    group = lax.axis_index("group")
    n_curve = lax.axis_size("curve")
    n_group = lax.axis_size("group")
    core = lax.rem(group, 2)
    ahead = (lax.rem(curve + 1, n_curve), group)
    behind = (lax.rem(curve + n_curve - 1, n_curve), group)
    above = (curve, lax.rem(group + 1, n_group))
    below = (curve, lax.rem(group + n_group - 1, n_group))

    def load_coarse(field, part, begin, count):
        source = (coarse_state_ref, coarse_kappa_ref)[field]
        return pltpu.make_async_copy(
            source.at[pl.ds(begin, count)],
            coarse.at[field, pl.ds(begin + 1, count)],
            coarse_sem.at[field, part],
        )

    def load_cells(patch):
        return pltpu.make_async_copy(state_ref.at[patch], cells.at[patch], cell_sem.at[patch])

    def load_table():
        return pltpu.make_async_copy(lanes_ref, lane_mats, table_sem)

    parts = ((3, 4), (0, 3), (7, 3))
    for field in range(2):
        load_coarse(field, 0, *parts[0]).start()
    load_table().start()
    for patch in (4, 5):
        load_cells(patch).start()
    for part in (1, 2):
        for field in range(2):
            load_coarse(field, part, *parts[part]).start()
    for patch in (3, 6, 2, 7, 1, 8, 0, 9):
        load_cells(patch).start()

    barrier = pltpu.get_barrier_semaphore()
    for device in (above, below, ahead, behind):
        pl.semaphore_signal(barrier, inc=1, device_id=device, device_id_type=MESH)

    faces[...] = jnp.zeros_like(faces)

    lane = lane_iota(SPEC)
    row_of = (lane % 64) // 8

    def pack(slot, patches, first):
        for tile in range(TILES):
            up = jnp.zeros((SPEC, 128), jnp.float32)
            down = jnp.zeros((SPEC, 128), jnp.float32)
            for place, patch in enumerate(patches):
                for field in range(2):
                    j = (first + place) * 2 + field
                    values = coarse[field, patch + 1, :, tile * 128 : (tile + 1) * 128]
                    up = jnp.where(row_of == 7 - j, pltpu.roll(values, (128 - 8 * j) % 128, 1), up)
                    down = jnp.where(row_of == j, pltpu.roll(values, 8 * j, 1), down)
            pack_out[0, slot, :, tile * 128 : (tile + 1) * 128] = up
            pack_out[1, slot, :, tile * 128 : (tile + 1) * 128] = down

    def pack_copy(way, slot):
        return pltpu.make_async_remote_copy(
            src_ref=pack_out.at[way, slot],
            dst_ref=pack_in.at[way, slot],
            send_sem=pack_send.at[way, slot],
            recv_sem=pack_recv.at[way, slot],
            device_id=(above, below)[way],
            device_id_type=MESH,
        )

    def toward(way):
        return (jnp.where(way == 0, ahead[0], behind[0]), group)

    def leaving(way, k):
        return jnp.where(way == 0, HALF + k, HALF - 1 - k)

    def edge_copy(way):
        return pltpu.make_async_remote_copy(
            src_ref=edge_out.at[way],
            dst_ref=edge_in.at[way],
            send_sem=edge_send.at[way],
            recv_sem=edge_recv.at[way],
            device_id=(ahead, behind)[way],
            device_id_type=MESH,
        )

    def move_copy(way, k, chunk):
        part = pl.ds(chunk * CHUNK, CHUNK)
        return pltpu.make_async_remote_copy(
            src_ref=own_ref.at[leaving(way, k), part],
            dst_ref=moved_ref.at[way, jnp.where(way == 0, k, HALF - 1 - k), part],
            send_sem=move_send.at[way, k, chunk],
            recv_sem=move_recv.at[way, k, chunk],
            device_id=toward(way),
            device_id_type=MESH,
        )

    def sends(way):
        return jnp.where(way == 0, curve < n_curve - 1, curve > 0)

    def gets(way):
        return jnp.where(way == 0, curve > 0, curve < n_curve - 1)

    def send_move(way, k, chunk):
        @pl.when(sends(way))
        def _():
            move_copy(way, k, chunk).start()

    def fix_copy(way):
        return pltpu.make_async_remote_copy(
            src_ref=fix_out.at[way],
            dst_ref=fix_in.at[way],
            send_sem=fix_send.at[way],
            recv_sem=fix_recv.at[way],
            device_id=toward(way),
            device_id_type=MESH,
        )

    def stage(slot):
        for field in range(2):
            for tile in range(TILES):
                values = coarse[field, slot, :, tile * 128 : (tile + 1) * 128]
                for i, rows in enumerate(split_pair(values)):
                    put_rows(staged.at[field, slot], 2 * tile + i - 1, rows)

    def stage_faces(slot):
        for tile in range(TILES):
            values = coarse[1, slot, :, tile * 128 : (tile + 1) * 128]
            for i, rows in enumerate(split_pair(values)):
                put_rows(outer.at[0], 2 * tile + i, rows)
                put_rows(outer.at[1], 2 * tile + i - 2, rows)
        faces[0:SPEC, :] = split_pair(coarse[0, slot, :, 0:128])[0]
        faces[PITCH : PITCH + SPEC, :] = split_pair(coarse[0, slot, :, COARSE - 128 : COARSE])[1]

    def dot(a, first, count):
        table = lane_mats[first * 128 : (first + count) * 128, :]
        return jnp.dot(a, table, preferred_element_type=jnp.float32)

    def keep(way, index, values, begins=(0, 1)):
        for half in range(2):
            part = values[:, half * 128 : (half + 1) * 128]
            for begin in begins:
                weights.at[way, index, half][pl.ds(begin, FLAT, stride=2), :] = part

    def spread(way, patch):
        z = lane_iota(FLAT) % 8

        def across(field):
            low, high = staged[field, patch], staged[field, patch + 2]
            return jnp.where(z == 7, low, jnp.where(z == 0, high, 0.0)).astype(jnp.bfloat16)

        own = staged[1, patch + 1].astype(jnp.bfloat16)

        def beside(values):
            return jnp.concatenate([own, values], axis=1)

        keep(way, 0, dot(own, 8, 1))
        for side in range(2):
            keep(way, 1, dot(beside(outer[side].astype(jnp.bfloat16)), 0, 2), (side,))
        keep(way, 3, dot(beside(across(1)), 4, 2))
        keep(way, 5, dot(across(0), 7, 1))
        edge = dot(faces[...].astype(jnp.bfloat16), 8, 1)
        for half in range(2):
            face_rows[way, half] = edge[:, half * 128 : (half + 1) * 128]

    def spread_y(way, patch, closed):
        own = staged[1, patch + 1].astype(jnp.bfloat16)
        if closed:
            keep(way, 2, dot(own, 2, 1))
        else:
            beside = jnp.concatenate([own, sides[1].astype(jnp.bfloat16)], axis=1)
            keep(way, 2, dot(beside, 2, 2))
            keep(way, 4, dot(sides[0].astype(jnp.bfloat16), 6, 1))

    def diffuse(way, patch, chunk, closed=False):
        row = lax.broadcasted_iota(jnp.int32, (8, 128), 0)
        lanes = lax.broadcasted_iota(jnp.int32, (8, 128), 1)
        odd_x, odd_y, odd_z = row % 2 == 1, (lanes // EDGE) % 2 == 1, lanes % 2 == 1
        first_x, last_x = row == 0, row == 7
        first_y, last_y = lanes < EDGE, lanes >= 128 - EDGE
        face_z = (lanes % EDGE == 0) | (lanes % EDGE == EDGE - 1)

        def one(species):
            begin = pl.multiple_of(species * EDGE, EDGE)
            p = [
                [
                    cells[patch, species, 8 * h : 8 * h + 8, 128 * v : 128 * v + 128]
                    for v in range(2)
                ]
                for h in range(2)
            ]
            down_x = [[pltpu.roll(p[h][v], 1, 0) for v in range(2)] for h in range(2)]
            up_x = [[pltpu.roll(p[h][v], 7, 0) for v in range(2)] for h in range(2)]
            down_y = [[pltpu.roll(p[h][v], EDGE, 1) for v in range(2)] for h in range(2)]
            up_y = [[pltpu.roll(p[h][v], 128 - EDGE, 1) for v in range(2)] for h in range(2)]
            for h in range(2):
                for v in range(2):
                    own = p[h][v]

                    def load(index, h=h, v=v):
                        return weights[way, index, v, pl.ds(begin + 8 * h, 8), :]

                    outside = face_rows[way, v, pl.ds(species + PITCH * h, 1), :]
                    dx, ux, dy, uy = down_x[h][v], up_x[h][v], down_y[h][v], up_y[h][v]
                    dz, uz = pltpu.roll(own, 1, 1), pltpu.roll(own, 127, 1)
                    inner = jnp.where(odd_x, dx, ux) + jnp.where(odd_y, dy, uy)
                    inner = inner + jnp.where(odd_z, dz, uz)
                    far_x = jnp.where(odd_x, ux, dx)
                    far_y = jnp.where(odd_y, uy, dy)
                    if h == 0:
                        far_x = jnp.where(first_x, outside, jnp.where(last_x, up_x[1][v], far_x))
                    else:
                        far_x = jnp.where(last_x, outside, jnp.where(first_x, down_x[0][v], far_x))
                    y_outside = own if closed else load(4)
                    if v == 0:
                        far_y = jnp.where(first_y, y_outside, jnp.where(last_y, up_y[h][1], far_y))
                    else:
                        far_y = jnp.where(last_y, y_outside, jnp.where(first_y, down_y[h][0], far_y))
                    far_z = jnp.where(face_z, load(5), jnp.where(odd_z, uz, dz))
                    change = load(0) * (inner - 3.0 * own)
                    change = change + load(1) * (far_x - own)
                    change = change + load(2) * (far_y - own)
                    change = change + load(3) * (far_z - own)
                    own_ref[patch, species, 8 * h : 8 * h + 8, 128 * v : 128 * v + 128] = own + change

        def block(b, carry):
            for i in range(BLOCK):
                one(chunk * CHUNK + b * BLOCK + i)
            return carry

        lax.fori_loop(0, CHUNK // BLOCK, block, 0)

    lanes8 = lax.broadcasted_iota(jnp.int32, (8, 128), 1)
    group8 = lax.rem(lanes8 + EDGE, 128) // 32

    def fix(way, patch):
        low, high = lanes8 < EDGE, lanes8 >= 128 - EDGE
        packed = None
        for n in range(2 * EARLY * CHUNK):
            species, h, j = n // 2, n % 2, n % 4
            terms = []
            for v in range(2):
                at = slice(species * EDGE + 8 * h, species * EDGE + 8 * h + 8)
                own = cells[patch, species, 8 * h : 8 * h + 8, 128 * v : 128 * v + 128]
                terms.append(weights[way, 2, v, at, :] * (weights[way, 4, v, at, :] - own))
            term = jnp.where(low, terms[0], jnp.where(high, terms[1], 0.0))
            if j == 0:
                packed = term
            else:
                packed = jnp.where(group8 == j, pltpu.roll(term, 32 * j, 1), packed)
            if j == 3:
                fix_out[way, 2 * (n - 3) : 2 * (n - 3) + 8, :] = packed

    def apply_fix(way, source, target, patch):
        for n in range(2 * EARLY * CHUNK):
            species, h, j = n // 2, n % 2, n % 4
            term = source[way, 2 * (n - j) : 2 * (n - j) + 8, :]
            if j:
                term = pltpu.roll(term, 128 - 32 * j, 1)
            for v in range(2):
                lanes = slice(128 * v, 128 * v + 128)
                inside = lanes8 < EDGE if v == 0 else lanes8 >= 128 - EDGE
                old = target[patch, species, 8 * h : 8 * h + 8, lanes]
                target[patch, species, 8 * h : 8 * h + 8, lanes] = old + jnp.where(inside, term, 0.0)

    def smooth(way, k):
        patch = leaving(way, k)
        slot = (k + 1) // 2
        base = 2 * lax.rem(k + 1, 2) + way

        @pl.when(k > 0)
        def _():
            stage_faces(patch + 1)
            spread(way, patch)

        for field in range(2):
            j = base * 2 + field
            back = 8 * j
            forth = lax.rem(128 - 8 * j, 128)
            for tile in range(TILES):
                part = slice(tile * 128, (tile + 1) * 128)
                low = pltpu.roll(pack_in[0, slot, :, part], back, 1)
                high = pltpu.roll(pack_in[1, slot, :, part], forth, 1)
                values = jnp.where(row_of == 7, low, jnp.where(row_of == 0, high, 0.0))
                for i, rows in enumerate(split_pair(values)):
                    put_rows(sides.at[field], 2 * tile + i - 1, rows)
        spread_y(way, patch, False)

        @pl.when(k > 0)
        def _():
            load_cells(patch).wait()
            for chunk in range(EARLY):
                diffuse(way, patch, chunk)
                send_move(way, k, chunk)

        for chunk in range(EARLY, CHUNKS):
            diffuse(way, patch, chunk)
            send_move(way, k, chunk)

        @pl.when(k == 0)
        def _():
            fix(way, patch)

            @pl.when(sends(way))
            def _():
                fix_copy(way).start()

    for field in range(2):
        load_coarse(field, 0, *parts[0]).wait()
    for slot in (5, 6, 7, 4):
        stage(slot)
    load_table().wait()
    for turn in range(2):
        way = 1 - turn
        patch = leaving(way, 0)
        stage_faces(patch + 1)
        spread(way, patch)
        spread_y(way, patch, True)
        load_cells(patch).wait()
        diffuse(way, patch, 0, closed=True)
    pack(0, (5, 4), 2)
    pl.semaphore_wait(barrier, 4)
    send_move(1, 0, 0)
    for side in range(2):
        pack_copy(side, 0).start()
    send_move(0, 0, 0)
    for part in (1, 2):
        for field in range(2):
            load_coarse(field, part, *parts[part]).wait()
    pack(1, (6, 3, 7, 2), 0)

    def send_packs(when, slot):
        @pl.when(when)
        def _():
            for side in range(2):
                pack_copy(side, slot).start()

    send_packs(core == 0, 1)
    for chunk in range(1, EARLY):
        for turn in range(2):
            way = 1 - turn
            diffuse(way, leaving(way, 0), chunk, closed=True)
            send_move(way, 0, chunk)
            if chunk + turn == 1:
                send_packs(core == 1, 1)

    def step(m, carry):
        k = m // 2
        for slot, turn in ((0, 0), (1, 2), (2, 6)):

            @pl.when(m == turn)
            def _(slot=slot):
                for way in range(2):
                    pack_copy(way, slot).wait_recv()

        @pl.when(m == 6)
        def _():
            for way in range(2):

                @pl.when(sends(way))
                def _(way=way):
                    for chunk in range(EARLY):
                        move_copy(way, 0, chunk).wait_send()

                apply_fix(way, fix_out, own_ref, 5 - way)

                @pl.when(gets(way))
                def _(way=way):
                    for chunk in range(EARLY):
                        move_copy(way, 0, chunk).wait_recv()
                    fix_copy(way).wait_recv()
                    apply_fix(way, fix_in, moved_ref.at[way], 4 * way)

        @pl.when(m == 8)
        def _():
            for way in range(2):
                edge_copy(way).wait_recv()
            for field in range(2):
                for tile in range(TILES):
                    part = slice(tile * 128, (tile + 1) * 128)
                    places = [4 * field + max(tile - 1, 0), 4 * field + min(tile, 3)]
                    for side, slot, begin in ((0, 0, 71), (1, PATCHES + 1, 64)):
                        low, high = (pltpu.roll(edge_in[side], begin - place, 1) for place in places)
                        coarse[field, slot, :, part] = jnp.where(lane < 64, low, high)

        @pl.when((m > 1) & (lax.rem(m, 2) == 0))
        def _():
            stage(7 + k)
            stage(4 - k)

        smooth(1 - lax.rem(m, 2), k)

        @pl.when(m == 1)
        def _():
            pack(2, (8, 1, 9, 0), 0)
            up = jnp.zeros((SPEC, 128), jnp.float32)
            down = jnp.zeros((SPEC, 128), jnp.float32)
            for place in range(8):
                field, tile = place // 4, place % 4

                def halves(patch, shift, field=field, tile=tile):
                    low, high = (
                        coarse[field, patch + 1, :, t * 128 : (t + 1) * 128] for t in (tile, tile + 1)
                    )
                    return jnp.where(lane < 64, pltpu.roll(low, shift, 1), pltpu.roll(high, shift, 1))

                here = lane % 8 == place
                up = jnp.where(here, halves(PATCHES - 1, 57 + place), up)
                down = jnp.where(here, halves(0, 64 + place), down)
            edge_out[0] = up
            edge_out[1] = down
            for way in range(2):
                edge_copy(way).start()

        send_packs(m == 1 + core, 2)
        return carry

    lax.fori_loop(0, 2 * HALF, step, 0)

    for way in range(2):
        for slot in range(3):
            pack_copy(way, slot).wait_send()
        edge_copy(way).wait_send()

        @pl.when(sends(way))
        def _(way=way):
            fix_copy(way).wait_send()
            for k in range(HALF):
                for chunk in range(EARLY if k == 0 else 0, CHUNKS):
                    move_copy(way, k, chunk).wait_send()

        @pl.when(gets(way))
        def _(way=way):
            for k in range(HALF):
                for chunk in range(EARLY if k == 0 else 0, CHUNKS):
                    move_copy(way, k, chunk).wait_recv()


def place_kernel(shift_ref, own_ref, moved_ref, out_ref, zeros, sem):
    curve = lax.axis_index("curve")
    here = shift_ref[0, curve]
    before = jnp.where(curve > 0, shift_ref[0, jnp.maximum(curve - 1, 0)], 0)
    count = PATCHES + here - before
    zeros[...] = jnp.zeros_like(zeros)
    for slot in range(2 * PATCHES):
        position = before + slot
        used = slot < count
        target = out_ref.at[slot]

        def put(source):
            pltpu.make_async_copy(source, target, sem).start()

        @pl.when(used & (position < 0))
        def _():
            put(moved_ref.at[0, jnp.clip(position + HALF, 0, HALF - 1)])

        @pl.when(used & (position >= PATCHES))
        def _():
            put(moved_ref.at[1, jnp.clip(position - PATCHES, 0, HALF - 1)])

        @pl.when(used & (position >= 0) & (position < PATCHES))
        def _():
            put(own_ref.at[jnp.clip(position, 0, PATCHES - 1)])

        @pl.when(jnp.logical_not(used))
        def _():
            put(zeros)

    pltpu.make_async_copy(out_ref, out_ref, sem).wait()


def shards(state, coarse_state, coarse_kappa, bound_shift):
    f32, bf16 = jnp.float32, jnp.bfloat16
    patch = (SPEC, EDGE, LANES)
    hbm = pl.BlockSpec(memory_space=pltpu.HBM)
    vmem = pl.BlockSpec(memory_space=pltpu.VMEM)
    lane_table = jnp.asarray(lane_tables(), bf16)
    operands = (state, coarse_state, coarse_kappa, lane_table)
    own, moved = pl.pallas_call(
        exchange_kernel,
        name="exchange",
        out_shape=[
            jax.ShapeDtypeStruct((PATCHES,) + patch, f32),
            jax.ShapeDtypeStruct((2, HALF) + patch, f32),
        ],
        in_specs=[hbm] * 4,
        out_specs=[vmem] * 2,
        scratch_shapes=[
            pltpu.VMEM((PATCHES,) + patch, f32),
            pltpu.VMEM((2, PATCHES + 2, SPEC, COARSE), f32),
            pltpu.VMEM(lane_table.shape, bf16),
            pltpu.VMEM((2, PATCHES + 2, FLAT, 128), f32),
            pltpu.VMEM((2, FLAT, 128), f32),
            pltpu.VMEM((2, FLAT, 128), f32),
            pltpu.VMEM((2 * PITCH, 128), f32),
            pltpu.VMEM((2, 2, 2 * PITCH, 128), f32),
            pltpu.VMEM((2, 3, SPEC, COARSE), f32),
            pltpu.VMEM((2, 3, SPEC, COARSE), f32),
            pltpu.VMEM((2, SPEC, 128), f32),
            pltpu.VMEM((2, SPEC, 128), f32),
            pltpu.VMEM((2, 6, 2, 2 * FLAT, 128), f32),
            pltpu.VMEM((2, 4 * EARLY * CHUNK, 128), f32),
            pltpu.VMEM((2, 4 * EARLY * CHUNK, 128), f32),
            pltpu.SemaphoreType.DMA((PATCHES,)),
            pltpu.SemaphoreType.DMA((2, 3)),
            pltpu.SemaphoreType.DMA,
            pltpu.SemaphoreType.DMA((2, 3)),
            pltpu.SemaphoreType.DMA((2, 3)),
            pltpu.SemaphoreType.DMA((2,)),
            pltpu.SemaphoreType.DMA((2,)),
            pltpu.SemaphoreType.DMA((2, HALF, CHUNKS)),
            pltpu.SemaphoreType.DMA((2, HALF, CHUNKS)),
            pltpu.SemaphoreType.DMA((2,)),
            pltpu.SemaphoreType.DMA((2,)),
        ],
        compiler_params=pltpu.CompilerParams(
            collective_id=0, has_side_effects=True, vmem_limit_bytes=36 << 20
        ),
        cost_estimate=pl.CostEstimate(flops=8 << 30, bytes_accessed=12 << 20, transcendentals=0),
    )(*(pltpu.with_memory_space_constraint(v, pltpu.HBM) for v in operands))
    return pl.pallas_call(
        place_kernel,
        name="place",
        out_shape=jax.ShapeDtypeStruct((2 * PATCHES,) + patch, f32),
        in_specs=[pl.BlockSpec(memory_space=pltpu.SMEM)] + [vmem] * 2,
        out_specs=hbm,
        scratch_shapes=[pltpu.VMEM(patch, f32), pltpu.SemaphoreType.DMA],
        compiler_params=pltpu.CompilerParams(vmem_limit_bytes=16 << 20),
        cost_estimate=pl.CostEstimate(flops=0, bytes_accessed=7 << 20, transcendentals=0),
    )(bound_shift, own, moved)


def solution(mesh):
    in_specs = (
        P(("curve", "group"), None, None, None),
        P(("curve", "group"), None, None),
        P(("curve", "group"), None, None),
        P("group", None),
    )
    out_specs = P(("curve", "group"), None, None, None)
    return jax.shard_map(shards, mesh=mesh, in_specs=in_specs, out_specs=out_specs, check_vma=False)
```

```python
import jax
import jax.numpy as jnp
import numpy as np
from jax import lax
from jax.experimental import pallas as pl
from jax.experimental.pallas import tpu as pltpu
from jax.sharding import PartitionSpec as P

MESH = pl.DeviceIdType.MESH
SPEC = 20
EDGE = 16
LANES = EDGE * EDGE
PATCHES = 10
HALF = 5
COARSE = 640
PITCH = 24
TILES = COARSE // 128
CHUNK = 10
CHUNKS = SPEC // CHUNK
BLOCK = 2
EARLY = 2
FLAT = SPEC * 8
ROOM = PITCH * 8


def lane_tables():
    half = np.zeros((64, LANES), np.float32)
    y_own, y_side, y_face = np.zeros_like(half), np.zeros_like(half), np.zeros_like(half)
    z_own, z_side, z_face = np.zeros_like(half), np.zeros_like(half), np.zeros_like(half)
    for r in range(EDGE):
        for q in range(EDGE):
            lane, cy, cz = r * EDGE + q, r // 2, q // 2
            here = cy * 8 + cz
            half[here, lane] = 0.5
            y_own[here, lane] += 0.5
            z_own[here, lane] += 0.5
            near = r + 1 if r % 2 else r - 1
            if near < 0:
                y_side[56 + cz, lane], y_face[56 + cz, lane] = 0.5, 1.0
            elif near >= EDGE:
                y_side[cz, lane], y_face[cz, lane] = 0.5, 1.0
            else:
                y_own[near // 2 * 8 + cz, lane] += 0.5
            near = q + 1 if q % 2 else q - 1
            if near < 0:
                z_side[cy * 8 + 7, lane], z_face[cy * 8 + 7, lane] = 0.5, 1.0
            elif near >= EDGE:
                z_side[cy * 8, lane], z_face[cy * 8, lane] = 0.5, 1.0
            else:
                z_own[cy * 8 + near // 2, lane] += 0.5
    parts = [half, half, y_own, y_side, z_own, z_side, y_face, z_face, 2.0 * half]
    return np.concatenate([np.concatenate([part, part]) for part in parts])


def lane_iota(rows):
    return lax.broadcasted_iota(jnp.int32, (rows, 128), 1)


def split_pair(values):
    lane = lane_iota(SPEC)
    high = values.astype(jnp.bfloat16).astype(jnp.float32)
    rest = values - high
    even = jnp.where(lane < 64, high, pltpu.roll(rest, 64, 1))
    odd = jnp.where(lane < 64, pltpu.roll(high, 64, 1), rest)
    return even, odd


def put_rows(target, place, values):
    if 0 <= place < 8:
        target[pl.ds(place, SPEC, stride=8), :] = values


def exchange_kernel(
    state_ref,
    coarse_state_ref,
    coarse_kappa_ref,
    lanes_ref,
    own_ref,
    moved_ref,
    cells,
    coarse,
    lane_mats,
    staged,
    outer,
    sides,
    faces,
    face_rows,
    pack_out,
    pack_in,
    edge_out,
    edge_in,
    weights,
    fix_out,
    fix_in,
    cell_sem,
    coarse_sem,
    table_sem,
    pack_send,
    pack_recv,
    edge_send,
    edge_recv,
    move_send,
    move_recv,
    fix_send,
    fix_recv,
):
    curve = lax.axis_index("curve")
    group = lax.axis_index("group")
    n_curve = lax.axis_size("curve")
    n_group = lax.axis_size("group")
    core = lax.rem(group, 2)
    ahead = (lax.rem(curve + 1, n_curve), group)
    behind = (lax.rem(curve + n_curve - 1, n_curve), group)
    above = (curve, lax.rem(group + 1, n_group))
    below = (curve, lax.rem(group + n_group - 1, n_group))

    def load_coarse(field, part, begin, count):
        source = (coarse_state_ref, coarse_kappa_ref)[field]
        return pltpu.make_async_copy(
            source.at[pl.ds(begin, count)],
            coarse.at[field, pl.ds(begin + 1, count)],
            coarse_sem.at[field, part],
        )

    def load_cells(patch):
        return pltpu.make_async_copy(state_ref.at[patch], cells.at[patch], cell_sem.at[patch])

    def load_table():
        return pltpu.make_async_copy(lanes_ref, lane_mats, table_sem)

    parts = ((3, 4), (0, 3), (7, 3))
    for field in range(2):
        load_coarse(field, 0, *parts[0]).start()
    load_table().start()
    for patch in (4, 5):
        load_cells(patch).start()
    for part in (1, 2):
        for field in range(2):
            load_coarse(field, part, *parts[part]).start()
    for patch in (3, 6, 2, 7, 1, 8, 0, 9):
        load_cells(patch).start()

    barrier = pltpu.get_barrier_semaphore()
    for device in (above, below, ahead, behind):
        pl.semaphore_signal(barrier, inc=1, device_id=device, device_id_type=MESH)

    faces[...] = jnp.zeros_like(faces)

    lane = lane_iota(SPEC)
    row_of = (lane % 64) // 8

    def pack(slot, patches, first):
        for tile in range(TILES):
            up = jnp.zeros((SPEC, 128), jnp.float32)
            down = jnp.zeros((SPEC, 128), jnp.float32)
            for place, patch in enumerate(patches):
                for field in range(2):
                    j = (first + place) * 2 + field
                    values = coarse[field, patch + 1, :, tile * 128 : (tile + 1) * 128]
                    up = jnp.where(row_of == 7 - j, pltpu.roll(values, (128 - 8 * j) % 128, 1), up)
                    down = jnp.where(row_of == j, pltpu.roll(values, 8 * j, 1), down)
            pack_out[0, slot, :, tile * 128 : (tile + 1) * 128] = up
            pack_out[1, slot, :, tile * 128 : (tile + 1) * 128] = down

    def pack_copy(way, slot):
        return pltpu.make_async_remote_copy(
            src_ref=pack_out.at[way, slot],
            dst_ref=pack_in.at[way, slot],
            send_sem=pack_send.at[way, slot],
            recv_sem=pack_recv.at[way, slot],
            device_id=(above, below)[way],
            device_id_type=MESH,
        )

    def toward(way):
        return (jnp.where(way == 0, ahead[0], behind[0]), group)

    def leaving(way, k):
        return jnp.where(way == 0, HALF + k, HALF - 1 - k)

    def edge_copy(way):
        return pltpu.make_async_remote_copy(
            src_ref=edge_out.at[way],
            dst_ref=edge_in.at[way],
            send_sem=edge_send.at[way],
            recv_sem=edge_recv.at[way],
            device_id=(ahead, behind)[way],
            device_id_type=MESH,
        )

    def move_copy(way, k, chunk):
        part = pl.ds(chunk * CHUNK, CHUNK)
        return pltpu.make_async_remote_copy(
            src_ref=own_ref.at[leaving(way, k), part],
            dst_ref=moved_ref.at[way, jnp.where(way == 0, k, HALF - 1 - k), part],
            send_sem=move_send.at[way, k, chunk],
            recv_sem=move_recv.at[way, k, chunk],
            device_id=toward(way),
            device_id_type=MESH,
        )

    def sends(way):
        return jnp.where(way == 0, curve < n_curve - 1, curve > 0)

    def gets(way):
        return jnp.where(way == 0, curve > 0, curve < n_curve - 1)

    def send_move(way, k, chunk):
        @pl.when(sends(way))
        def _():
            move_copy(way, k, chunk).start()

    def fix_copy(way):
        return pltpu.make_async_remote_copy(
            src_ref=fix_out.at[way],
            dst_ref=fix_in.at[way],
            send_sem=fix_send.at[way],
            recv_sem=fix_recv.at[way],
            device_id=toward(way),
            device_id_type=MESH,
        )

    def stage(slot):
        for field in range(2):
            for tile in range(TILES):
                values = coarse[field, slot, :, tile * 128 : (tile + 1) * 128]
                for i, rows in enumerate(split_pair(values)):
                    put_rows(staged.at[field, slot], 2 * tile + i - 1, rows)

    def stage_faces(slot):
        for tile in range(TILES):
            values = coarse[1, slot, :, tile * 128 : (tile + 1) * 128]
            for i, rows in enumerate(split_pair(values)):
                put_rows(outer.at[0], 2 * tile + i, rows)
                put_rows(outer.at[1], 2 * tile + i - 2, rows)
        faces[0:SPEC, :] = split_pair(coarse[0, slot, :, 0:128])[0]
        faces[PITCH : PITCH + SPEC, :] = split_pair(coarse[0, slot, :, COARSE - 128 : COARSE])[1]

    def dot(a, first, count):
        table = lane_mats[first * 128 : (first + count) * 128, :]
        return jnp.dot(a, table, preferred_element_type=jnp.float32)

    def keep(way, index, values, begins=(0, 1)):
        for half in range(2):
            part = values[:, half * 128 : (half + 1) * 128]
            for begin in begins:
                weights.at[way, index, half][pl.ds(begin, FLAT, stride=2), :] = part

    def spread(way, patch):
        z = lane_iota(FLAT) % 8

        def across(field):
            low, high = staged[field, patch, 0:FLAT], staged[field, patch + 2, 0:FLAT]
            return jnp.where(z == 7, low, jnp.where(z == 0, high, 0.0)).astype(jnp.bfloat16)

        own = staged[1, patch + 1, 0:FLAT].astype(jnp.bfloat16)

        def beside(values):
            return jnp.concatenate([own, values], axis=1)

        keep(way, 0, dot(own, 8, 1))
        for side in range(2):
            keep(way, 1, dot(beside(outer[side, 0:FLAT].astype(jnp.bfloat16)), 0, 2), (side,))
        keep(way, 3, dot(beside(across(1)), 4, 2))
        keep(way, 5, dot(across(0), 7, 1))
        edge = dot(faces[...].astype(jnp.bfloat16), 8, 1)
        for half in range(2):
            face_rows[way, half] = edge[:, half * 128 : (half + 1) * 128]

    def spread_y(way, patch, closed):
        own = staged[1, patch + 1, 0:FLAT].astype(jnp.bfloat16)
        if closed:
            keep(way, 2, dot(own, 2, 1))
        else:
            beside = jnp.concatenate([own, sides[1, 0:FLAT].astype(jnp.bfloat16)], axis=1)
            keep(way, 2, dot(beside, 2, 2))
            keep(way, 4, dot(sides[0, 0:FLAT].astype(jnp.bfloat16), 6, 1))

    def diffuse(way, patch, chunk, closed=False):
        row = lax.broadcasted_iota(jnp.int32, (8, 128), 0)
        lanes = lax.broadcasted_iota(jnp.int32, (8, 128), 1)
        odd_x, odd_y, odd_z = row % 2 == 1, (lanes // EDGE) % 2 == 1, lanes % 2 == 1
        first_x, last_x = row == 0, row == 7
        first_y, last_y = lanes < EDGE, lanes >= 128 - EDGE
        face_z = (lanes % EDGE == 0) | (lanes % EDGE == EDGE - 1)

        def one(species):
            begin = pl.multiple_of(species * EDGE, EDGE)
            p = [
                [
                    cells[patch, species, 8 * h : 8 * h + 8, 128 * v : 128 * v + 128]
                    for v in range(2)
                ]
                for h in range(2)
            ]
            down_x = [[pltpu.roll(p[h][v], 1, 0) for v in range(2)] for h in range(2)]
            up_x = [[pltpu.roll(p[h][v], 7, 0) for v in range(2)] for h in range(2)]
            down_y = [[pltpu.roll(p[h][v], EDGE, 1) for v in range(2)] for h in range(2)]
            up_y = [[pltpu.roll(p[h][v], 128 - EDGE, 1) for v in range(2)] for h in range(2)]
            for h in range(2):
                for v in range(2):
                    own = p[h][v]

                    def load(index, h=h, v=v):
                        return weights[way, index, v, pl.ds(begin + 8 * h, 8), :]

                    outside = face_rows[way, v, pl.ds(species + PITCH * h, 1), :]
                    dx, ux, dy, uy = down_x[h][v], up_x[h][v], down_y[h][v], up_y[h][v]
                    dz, uz = pltpu.roll(own, 1, 1), pltpu.roll(own, 127, 1)
                    inner = jnp.where(odd_x, dx, ux) + jnp.where(odd_y, dy, uy)
                    inner = inner + jnp.where(odd_z, dz, uz)
                    far_x = jnp.where(odd_x, ux, dx)
                    far_y = jnp.where(odd_y, uy, dy)
                    if h == 0:
                        far_x = jnp.where(first_x, outside, jnp.where(last_x, up_x[1][v], far_x))
                    else:
                        far_x = jnp.where(last_x, outside, jnp.where(first_x, down_x[0][v], far_x))
                    y_outside = own if closed else load(4)
                    if v == 0:
                        far_y = jnp.where(first_y, y_outside, jnp.where(last_y, up_y[h][1], far_y))
                    else:
                        far_y = jnp.where(last_y, y_outside, jnp.where(first_y, down_y[h][0], far_y))
                    far_z = jnp.where(face_z, load(5), jnp.where(odd_z, uz, dz))
                    change = load(0) * (inner - 3.0 * own)
                    change = change + load(1) * (far_x - own)
                    change = change + load(2) * (far_y - own)
                    change = change + load(3) * (far_z - own)
                    own_ref[patch, species, 8 * h : 8 * h + 8, 128 * v : 128 * v + 128] = own + change

        def block(b, carry):
            for i in range(BLOCK):
                one(chunk * CHUNK + b * BLOCK + i)
            return carry

        lax.fori_loop(0, CHUNK // BLOCK, block, 0)

    lanes8 = lax.broadcasted_iota(jnp.int32, (8, 128), 1)
    group8 = lax.rem(lanes8 + EDGE, 128) // 32

    def fix(way, patch):
        low, high = lanes8 < EDGE, lanes8 >= 128 - EDGE
        packed = None
        for n in range(2 * EARLY * CHUNK):
            species, h, j = n // 2, n % 2, n % 4
            terms = []
            for v in range(2):
                at = slice(species * EDGE + 8 * h, species * EDGE + 8 * h + 8)
                own = cells[patch, species, 8 * h : 8 * h + 8, 128 * v : 128 * v + 128]
                terms.append(weights[way, 2, v, at, :] * (weights[way, 4, v, at, :] - own))
            term = jnp.where(low, terms[0], jnp.where(high, terms[1], 0.0))
            if j == 0:
                packed = term
            else:
                packed = jnp.where(group8 == j, pltpu.roll(term, 32 * j, 1), packed)
            if j == 3:
                fix_out[way, 2 * (n - 3) : 2 * (n - 3) + 8, :] = packed

    def apply_fix(way, source, target, patch):
        for n in range(2 * EARLY * CHUNK):
            species, h, j = n // 2, n % 2, n % 4
            term = source[way, 2 * (n - j) : 2 * (n - j) + 8, :]
            if j:
                term = pltpu.roll(term, 128 - 32 * j, 1)
            for v in range(2):
                lanes = slice(128 * v, 128 * v + 128)
                inside = lanes8 < EDGE if v == 0 else lanes8 >= 128 - EDGE
                old = target[patch, species, 8 * h : 8 * h + 8, lanes]
                target[patch, species, 8 * h : 8 * h + 8, lanes] = old + jnp.where(inside, term, 0.0)

    def smooth(way, k):
        patch = leaving(way, k)
        slot = (k + 1) // 2
        base = 2 * lax.rem(k + 1, 2) + way

        @pl.when(k > 0)
        def _():
            stage_faces(patch + 1)
            spread(way, patch)

        for field in range(2):
            j = base * 2 + field
            back = 8 * j
            forth = lax.rem(128 - 8 * j, 128)
            for tile in range(TILES):
                part = slice(tile * 128, (tile + 1) * 128)
                low = pltpu.roll(pack_in[0, slot, :, part], back, 1)
                high = pltpu.roll(pack_in[1, slot, :, part], forth, 1)
                values = jnp.where(row_of == 7, low, jnp.where(row_of == 0, high, 0.0))
                for i, rows in enumerate(split_pair(values)):
                    put_rows(sides.at[field], 2 * tile + i - 1, rows)
        spread_y(way, patch, False)

        @pl.when(k > 0)
        def _():
            load_cells(patch).wait()
            for chunk in range(EARLY):
                diffuse(way, patch, chunk)
                send_move(way, k, chunk)

        for chunk in range(EARLY, CHUNKS):
            diffuse(way, patch, chunk)
            send_move(way, k, chunk)

        @pl.when(k == 0)
        def _():
            fix(way, patch)

            @pl.when(sends(way))
            def _():
                fix_copy(way).start()

    for field in range(2):
        load_coarse(field, 0, *parts[0]).wait()
    for slot in (5, 6, 7, 4):
        stage(slot)
    load_table().wait()
    for turn in range(2):
        way = 1 - turn
        patch = leaving(way, 0)
        stage_faces(patch + 1)
        spread(way, patch)
        spread_y(way, patch, True)
        load_cells(patch).wait()
        diffuse(way, patch, 0, closed=True)
    pack(0, (5, 4), 2)
    pl.semaphore_wait(barrier, 4)
    send_move(1, 0, 0)
    for side in range(2):
        pack_copy(side, 0).start()
    send_move(0, 0, 0)
    for part in (1, 2):
        for field in range(2):
            load_coarse(field, part, *parts[part]).wait()
    pack(1, (6, 3, 7, 2), 0)

    def send_packs(when, slot):
        @pl.when(when)
        def _():
            for side in range(2):
                pack_copy(side, slot).start()

    send_packs(core == 0, 1)
    for chunk in range(1, EARLY):
        for turn in range(2):
            way = 1 - turn
            diffuse(way, leaving(way, 0), chunk, closed=True)
            send_move(way, 0, chunk)
            if chunk + turn == 1:
                send_packs(core == 1, 1)

    def step(m, carry):
        k = m // 2
        for slot, turn in ((0, 0), (1, 2), (2, 6)):

            @pl.when(m == turn)
            def _(slot=slot):
                for way in range(2):
                    pack_copy(way, slot).wait_recv()

        @pl.when(m == 6)
        def _():
            for way in range(2):

                @pl.when(sends(way))
                def _(way=way):
                    for chunk in range(EARLY):
                        move_copy(way, 0, chunk).wait_send()

                apply_fix(way, fix_out, own_ref, 5 - way)

                @pl.when(gets(way))
                def _(way=way):
                    for chunk in range(EARLY):
                        move_copy(way, 0, chunk).wait_recv()
                    fix_copy(way).wait_recv()
                    apply_fix(way, fix_in, moved_ref.at[way], 4 * way)

        @pl.when(m == 8)
        def _():
            for way in range(2):
                edge_copy(way).wait_recv()
            for field in range(2):
                for tile in range(TILES):
                    part = slice(tile * 128, (tile + 1) * 128)
                    places = [4 * field + max(tile - 1, 0), 4 * field + min(tile, 3)]
                    for side, slot, begin in ((0, 0, 71), (1, PATCHES + 1, 64)):
                        low, high = (pltpu.roll(edge_in[side], begin - place, 1) for place in places)
                        coarse[field, slot, :, part] = jnp.where(lane < 64, low, high)

        @pl.when((m > 1) & (lax.rem(m, 2) == 0))
        def _():
            stage(7 + k)
            stage(4 - k)

        smooth(1 - lax.rem(m, 2), k)

        @pl.when(m == 1)
        def _():
            pack(2, (8, 1, 9, 0), 0)
            up = jnp.zeros((SPEC, 128), jnp.float32)
            down = jnp.zeros((SPEC, 128), jnp.float32)
            for place in range(8):
                field, tile = place // 4, place % 4

                def halves(patch, shift, field=field, tile=tile):
                    low, high = (
                        coarse[field, patch + 1, :, t * 128 : (t + 1) * 128] for t in (tile, tile + 1)
                    )
                    return jnp.where(lane < 64, pltpu.roll(low, shift, 1), pltpu.roll(high, shift, 1))

                here = lane % 8 == place
                up = jnp.where(here, halves(PATCHES - 1, 57 + place), up)
                down = jnp.where(here, halves(0, 64 + place), down)
            edge_out[0] = up
            edge_out[1] = down
            for way in range(2):
                edge_copy(way).start()

        send_packs(m == 1 + core, 2)
        return carry

    lax.fori_loop(0, 2 * HALF, step, 0)

    for way in range(2):
        for slot in range(3):
            pack_copy(way, slot).wait_send()
        edge_copy(way).wait_send()

        @pl.when(sends(way))
        def _(way=way):
            fix_copy(way).wait_send()
            for k in range(HALF):
                for chunk in range(EARLY if k == 0 else 0, CHUNKS):
                    move_copy(way, k, chunk).wait_send()

        @pl.when(gets(way))
        def _(way=way):
            for k in range(HALF):
                for chunk in range(EARLY if k == 0 else 0, CHUNKS):
                    move_copy(way, k, chunk).wait_recv()


def place_kernel(shift_ref, own_ref, moved_ref, out_ref, zeros, sem):
    curve = lax.axis_index("curve")
    here = shift_ref[0, curve]
    before = jnp.where(curve > 0, shift_ref[0, jnp.maximum(curve - 1, 0)], 0)
    count = PATCHES + here - before
    zeros[...] = jnp.zeros_like(zeros)
    for slot in range(2 * PATCHES):
        position = before + slot
        used = slot < count
        target = out_ref.at[slot]

        def put(source):
            pltpu.make_async_copy(source, target, sem).start()

        @pl.when(used & (position < 0))
        def _():
            put(moved_ref.at[0, jnp.clip(position + HALF, 0, HALF - 1)])

        @pl.when(used & (position >= PATCHES))
        def _():
            put(moved_ref.at[1, jnp.clip(position - PATCHES, 0, HALF - 1)])

        @pl.when(used & (position >= 0) & (position < PATCHES))
        def _():
            put(own_ref.at[jnp.clip(position, 0, PATCHES - 1)])

        @pl.when(jnp.logical_not(used))
        def _():
            put(zeros)

    pltpu.make_async_copy(out_ref, out_ref, sem).wait()


def shards(state, coarse_state, coarse_kappa, bound_shift):
    f32, bf16 = jnp.float32, jnp.bfloat16
    patch = (SPEC, EDGE, LANES)
    hbm = pl.BlockSpec(memory_space=pltpu.HBM)
    vmem = pl.BlockSpec(memory_space=pltpu.VMEM)
    lane_table = jnp.asarray(lane_tables(), bf16)
    operands = (state, coarse_state, coarse_kappa, lane_table)
    own, moved = pl.pallas_call(
        exchange_kernel,
        name="exchange",
        out_shape=[
            jax.ShapeDtypeStruct((PATCHES,) + patch, f32),
            jax.ShapeDtypeStruct((2, HALF) + patch, f32),
        ],
        in_specs=[hbm] * 4,
        out_specs=[vmem] * 2,
        scratch_shapes=[
            pltpu.VMEM((PATCHES,) + patch, f32),
            pltpu.VMEM((2, PATCHES + 2, SPEC, COARSE), f32),
            pltpu.VMEM(lane_table.shape, bf16),
            pltpu.VMEM((2, PATCHES + 2, ROOM, 128), f32),
            pltpu.VMEM((2, ROOM, 128), f32),
            pltpu.VMEM((2, ROOM, 128), f32),
            pltpu.VMEM((2 * PITCH, 128), f32),
            pltpu.VMEM((2, 2, 2 * PITCH, 128), f32),
            pltpu.VMEM((2, 3, SPEC, COARSE), f32),
            pltpu.VMEM((2, 3, SPEC, COARSE), f32),
            pltpu.VMEM((2, SPEC, 128), f32),
            pltpu.VMEM((2, SPEC, 128), f32),
            pltpu.VMEM((2, 6, 2, 2 * FLAT, 128), f32),
            pltpu.VMEM((2, 4 * EARLY * CHUNK, 128), f32),
            pltpu.VMEM((2, 4 * EARLY * CHUNK, 128), f32),
            pltpu.SemaphoreType.DMA((PATCHES,)),
            pltpu.SemaphoreType.DMA((2, 3)),
            pltpu.SemaphoreType.DMA,
            pltpu.SemaphoreType.DMA((2, 3)),
            pltpu.SemaphoreType.DMA((2, 3)),
            pltpu.SemaphoreType.DMA((2,)),
            pltpu.SemaphoreType.DMA((2,)),
            pltpu.SemaphoreType.DMA((2, HALF, CHUNKS)),
            pltpu.SemaphoreType.DMA((2, HALF, CHUNKS)),
            pltpu.SemaphoreType.DMA((2,)),
            pltpu.SemaphoreType.DMA((2,)),
        ],
        compiler_params=pltpu.CompilerParams(
            collective_id=0, has_side_effects=True, vmem_limit_bytes=36 << 20
        ),
        cost_estimate=pl.CostEstimate(flops=8 << 30, bytes_accessed=12 << 20, transcendentals=0),
    )(*(pltpu.with_memory_space_constraint(v, pltpu.HBM) for v in operands))
    return pl.pallas_call(
        place_kernel,
        name="place",
        out_shape=jax.ShapeDtypeStruct((2 * PATCHES,) + patch, f32),
        in_specs=[pl.BlockSpec(memory_space=pltpu.SMEM)] + [vmem] * 2,
        out_specs=hbm,
        scratch_shapes=[pltpu.VMEM(patch, f32), pltpu.SemaphoreType.DMA],
        compiler_params=pltpu.CompilerParams(vmem_limit_bytes=16 << 20),
        cost_estimate=pl.CostEstimate(flops=0, bytes_accessed=7 << 20, transcendentals=0),
    )(bound_shift, own, moved)


def solution(mesh):
    in_specs = (
        P(("curve", "group"), None, None, None),
        P(("curve", "group"), None, None),
        P(("curve", "group"), None, None),
        P("group", None),
    )
    out_specs = P(("curve", "group"), None, None, None)
    return jax.shard_map(shards, mesh=mesh, in_specs=in_specs, out_specs=out_specs, check_vma=False)
```
